256 devices in a mesh: dom: 64 (over x, z, core), sub: 4 (over y).
Axes of the slice: x: 4, y: 4, z: 8, core: 2. Of those that a mesh axis runs over, the one named last changes fastest.
Arguments:
- positions: float32 [3, 2097152], P(None, ('dom', 'sub')), may hold values from 0 to 1
- masses: float32 [2097152], P(('dom', 'sub')), may hold values from 0.00029296876 to 0.0029296875
- cell_mass: float32 [32768], P(('dom', 'sub')), may hold values from 0.00234375 to 0.0234375
- cell_center: float32 [3, 32768], P(None, ('dom', 'sub')), may hold values from 0 to 1
- cell_quad: float32 [6, 32768], P(None, ('dom', 'sub')), may hold values from -0.0046875 to 0.0046875
- cell_list: int32 [32768, 128], P(('dom', 'sub')), may hold values from 0 to 32767
- leaf_list: int32 [32768, 16], P(('dom', 'sub')), may hold values from 0 to 575, as said below
- send_list: int32 [64, 4, 8, 8], P('dom', 'sub'), may hold values from 0 to 127
- send_count: int32 [64, 4, 8], P('dom', 'sub'), may hold values from 1 to 8, as said below
Outputs:
- accel: float32 [3, 2097152], P(None, ('dom', 'sub'))
The draws below stay inside these ranges and needn't reach their ends.
Inputs may be any that keep to these rules, and one draw needn't show every extreme that they name: `send_count`: counts fall off with the distance along the curve: an offset of one domain always carries 8 blocks, an offset of d domains at most max(1, 8 // d). `leaf_list`: each id names a block of the group's own domain or a slot of the far part that carries a block.
All inputs are finite; a program needn't handle non-finite values.
Results may differ from the reference program's by a relative error of at most 0.0003.
Values sent between devices are 32-bit elements; how exact they have to be, the bound alone decides.
A program may use at most 128 MiB of HBM per device.

```python
import math
import jax
import jax.numpy as jnp
from jax import lax

LEAF = 64
LEAF_DEV = 128
NCELL = 128
NLEAF = 16
RANGE = 4
CAP = 8
PARTICLES = 2097152
CELLS = 32768
GROUPS = 32768
N_DOM = 64
N_SUB = 4


def curve_counts(key):
    offsets = jnp.concatenate([jnp.arange(-RANGE, 0, dtype=jnp.int32), jnp.arange(1, RANGE + 1, dtype=jnp.int32)])
    reach = jnp.abs(offsets)
    top = jnp.maximum(2, CAP // reach + 1)
    drawn = jax.random.randint(key, (N_DOM, N_SUB, 2 * RANGE), 1, top[None, None, :])
    return jnp.where(reach[None, None, :] == 1, CAP, drawn).astype(jnp.int32)


def draw_send_count(key, part):
    return curve_counts(key)


def draw_leaf_list(key, part):
    counts = curve_counts(key)
    key = jax.random.fold_in(key, 11)
    key_near, key_slot, key_pick, key_side = jax.random.split(key, 4)
    offsets = jnp.concatenate([jnp.arange(-RANGE, 0, dtype=jnp.int32), jnp.arange(1, RANGE + 1, dtype=jnp.int32)])
    groups = jnp.arange(GROUPS, dtype=jnp.int32)
    device = groups // LEAF_DEV
    domain = (device // N_SUB)[:, None]
    segment = (device % N_SUB)[:, None]
    near = jax.random.randint(key_near, (GROUPS, NLEAF), 0, N_SUB * LEAF_DEV)
    slot = jax.random.randint(key_slot, (GROUPS, NLEAF), 0, 2 * RANGE)
    source = domain - offsets[slot]
    bad = (source < 0) | (source >= N_DOM)
    slot = jnp.where(bad, 2 * RANGE - 1 - slot, slot)
    source = domain - offsets[slot]
    count = counts[source, jnp.broadcast_to(segment, slot.shape), slot]
    pick = jax.random.randint(key_pick, (GROUPS, NLEAF), 0, CAP) % count
    far = N_SUB * LEAF_DEV + slot * CAP + pick
    side = jax.random.randint(key_side, (GROUPS, NLEAF), 0, 2)
    return jnp.where(side == 1, far, near).astype(jnp.int32)


def set_ends(array, rng, smallest, high):
    longest = array.shape.index(max(array.shape))
    spots = []
    for shift in (0, 1):
        where = [jax.random.randint(jax.random.fold_in(rng, axis), (), 0, length) for axis, length in enumerate(array.shape)]
        where[longest] = (where[longest] + shift) % array.shape[longest]
        spots.append(tuple(where))
    return array.at[spots[0]].set(smallest).at[spots[1]].set(high)


def levels(key, shape, cuts, smallest, top_value):
    gain = 1.0
    for dim, parts in cuts:
        draws = jax.random.uniform(jax.random.fold_in(jax.random.fold_in(key, 6), dim), (parts,), jnp.float32, smallest / len(cuts), top_value / len(cuts))
        gain = gain * jnp.repeat(jnp.exp(draws), shape[dim] // parts).reshape((-1,) + (1,) * (len(shape) - 1 - dim))
    return gain


def noise(own_key, shape, spread, most, cuts=(), kind=jnp.bfloat16):
    array = jax.random.normal(own_key, shape, jnp.float32) * spread
    if len(cuts) > 0:
        array = levels(own_key, shape, cuts, -0.22, 0.18) * array
    return jnp.clip(array, min=-most, max=most).astype(kind)


def setup_inputs(seed: int = 0) -> dict:
    streams_of = jax.random.split(jax.random.key(seed), 10)
    return {
        "positions": jnp.clip(1.0 * jax.random.uniform(streams_of[0], (3, PARTICLES), jnp.float32) ** levels(streams_of[0], (3, PARTICLES), ((1, 256),), -0.2, 0.2), 0.0, 1.0),
        "masses": jnp.clip(jnp.exp(math.log(0.0029296875) - 2.3025851 * jax.random.uniform(streams_of[1], (PARTICLES,), jnp.float32) ** levels(streams_of[1], (PARTICLES,), ((0, 256),), -0.2, 0.2)), 0.00029296876, 0.0029296875),
        "cell_mass": jnp.clip(jnp.exp(math.log(0.0234375) - 2.3025851 * jax.random.uniform(streams_of[2], (CELLS,), jnp.float32) ** levels(streams_of[2], (CELLS,), ((0, 256),), -0.2, 0.2)), 0.00234375, 0.0234375),
        "cell_center": jnp.clip(1.0 * jax.random.uniform(streams_of[3], (3, CELLS), jnp.float32) ** levels(streams_of[3], (3, CELLS), ((1, 256),), -0.2, 0.2), 0.0, 1.0),
        "cell_quad": noise(streams_of[4], (6, CELLS), (0.1 / NCELL), 0.0046875, ((1, 256),), jnp.float32),
        "cell_list": set_ends(jax.random.randint(streams_of[5], (GROUPS, NCELL), 0, CELLS), jax.random.fold_in(streams_of[5], 1), 0, CELLS - 1).astype(jnp.int32),
        "leaf_list": draw_leaf_list(jax.random.fold_in(streams_of[9], 71), 0),
        "send_list": set_ends(jax.random.randint(streams_of[7], (N_DOM, N_SUB, 2 * RANGE, CAP), 0, LEAF_DEV), jax.random.fold_in(streams_of[7], 1), 0, LEAF_DEV - 1).astype(jnp.int32),
        "send_count": draw_send_count(jax.random.fold_in(streams_of[9], 71), 0),
    }


softening_sq = 0.0025

def direct_pull(targets, sources, weights):
    offset = sources[:, :, None, :] - targets[:, :, :, None]
    dist_sq = lax.optimization_barrier(jnp.sum(offset * offset, axis=0)) + softening_sq
    factor = weights[:, None, :] / (dist_sq * jnp.sqrt(dist_sq))
    return lax.optimization_barrier(jnp.sum(offset * factor[None], axis=-1))

def multipole_pull(targets, moments):
    offset = targets[:, :, :, None] - moments[1:4, :, None, :]
    dist_sq = lax.optimization_barrier(jnp.sum(offset * offset, axis=0)) + softening_sq
    inv_one = 1.0 / jnp.sqrt(dist_sq)
    inv_two = inv_one * inv_one
    inv_three = inv_one * inv_two
    inv_five = inv_three * inv_two
    inv_seven = inv_five * inv_two
    quad_part = moments[4:10, :, None, :]
    q_times_x = quad_part[0] * offset[0] + quad_part[3] * offset[1] + quad_part[4] * offset[2]
    q_times_y = quad_part[3] * offset[0] + quad_part[1] * offset[1] + quad_part[5] * offset[2]
    q_times_z = quad_part[4] * offset[0] + quad_part[5] * offset[1] + quad_part[2] * offset[2]
    q_times = jnp.stack([q_times_x, q_times_y, q_times_z])
    quad_form = lax.optimization_barrier(jnp.sum(offset * q_times, axis=0))
    mass_part = moments[0, :, None, :]
    accel_terms = -mass_part * inv_three * offset + inv_five * q_times - 2.5 * inv_seven * quad_form * offset
    return lax.optimization_barrier(jnp.sum(accel_terms, axis=-1))

def group_pull(targets, essential, leaf_ids, cell_table, cell_ids):
    groups_here = leaf_ids.shape[0]
    particle_ids = (leaf_ids[:, :, None] * LEAF + jnp.arange(LEAF, dtype=jnp.int32)[None, None, :]).reshape(groups_here, -1)
    picked = essential[:, particle_ids]
    moments = cell_table[:, cell_ids]
    return direct_pull(targets, picked[0:3], picked[3]) + multipole_pull(targets, moments)

def reference(positions, masses, cell_mass, cell_center, cell_quad, cell_list, leaf_list, send_list, send_count):
    packed = jnp.concatenate([positions, masses[None]], axis=0).reshape(4, N_DOM, N_SUB, LEAF_DEV * LEAF)
    cell_table = jnp.concatenate([cell_mass[None], cell_center, cell_quad], axis=0)
    cell_lists = cell_list.reshape(N_DOM, N_SUB, LEAF_DEV, NCELL)
    leaf_lists = leaf_list.reshape(N_DOM, N_SUB, LEAF_DEV, NLEAF)
    offsets = jnp.concatenate([jnp.arange(-RANGE, 0, dtype=jnp.int32), jnp.arange(1, RANGE + 1, dtype=jnp.int32)])
    slot_index = jnp.arange(2 * RANGE, dtype=jnp.int32)

    def one_domain(linear):
        domain = linear // N_SUB
        segment = linear % N_SUB
        nearby = packed[:, domain].reshape(4, N_SUB * LEAF_DEV * LEAF)
        column = packed[:, :, segment].reshape(4, N_DOM * LEAF_DEV * LEAF)
        source = domain - offsets
        inside = (source >= 0) & (source < N_DOM)
        clipped = jnp.clip(source, 0, N_DOM - 1).astype(jnp.int32)
        chosen = send_list[clipped, segment, slot_index, :]
        counts = send_count[clipped, segment, slot_index]
        live = inside[:, None] & (jnp.arange(CAP, dtype=jnp.int32)[None, :] < counts[:, None])
        block_ids = clipped[:, None] * LEAF_DEV + chosen
        flat_ids = (block_ids[:, :, None] * LEAF + jnp.arange(LEAF, dtype=jnp.int32)[None, None, :]).reshape(-1)
        weight = jnp.repeat(live.astype(jnp.float32).reshape(-1), LEAF)
        remote = column[:, flat_ids] * weight[None, :]
        essential = jnp.concatenate([nearby, remote], axis=1)
        targets = packed[0:3, domain, segment].reshape(3, LEAF_DEV, LEAF)
        pulled = group_pull(targets, essential, leaf_lists[domain, segment], cell_table, cell_lists[domain, segment])
        return pulled.reshape(3, LEAF_DEV * LEAF)
    result = lax.map(one_domain, jnp.arange(N_DOM * N_SUB, dtype=jnp.int32))
    return result.transpose(1, 0, 2).reshape(3, N_DOM * N_SUB * LEAF_DEV * LEAF)
```

```python
import functools

import jax
import jax.numpy as jnp
from jax import lax
from jax.experimental import pallas as pl
from jax.experimental.pallas import tpu as pltpu
from jax.sharding import PartitionSpec as P

LEAF = 64
NCELL = 128
NLEAF = 16
RANGE = 4
CAP = 8
EPS = 0.0025
F32 = jnp.float32
BF16 = jnp.bfloat16
MESH = pl.DeviceIdType.MESH

NX, NY, NZ, NCORE = 4, 4, 8, 2
SIZES = {"x": NX, "y": NY, "z": NZ}
ROWS = 16
PARTS = ((0, 6, ("z", "x", "y")), (6, 5, ("x", "y", "z")), (11, 5, ("y", "z", "x")))
OFFSETS = tuple(range(-RANGE, 0)) + tuple(range(1, RANGE + 1))
PAIRS = 64
ALL_PAIRS = NY * PAIRS + len(OFFSETS) * CAP // 2
N_CELL_ROWS = NX * NY * NZ * NCORE * ROWS


def exchange_kernel(
    pos_ref, mass_ref, cmass_ref, ccen_ref, cquad_ref, send_list, send_count,
    leaf_ref, table_ref,
    pad, own, far_out, near_send, near_recv, far_send, far_recv, cell_send, cell_recv, core_send, core_recv,
):
    dom = lax.axis_index("dom")
    sub = lax.axis_index("sub")
    core = dom % NCORE
    at = {"x": dom // (NZ * NCORE), "z": (dom // NCORE) % NZ, "y": sub}

    def device(x, y, z, c):
        return ((x * NZ + z) * NCORE + c, y)

    def peer(axis, step):
        where = dict(at)
        where[axis] = (at[axis] + step) % SIZES[axis]
        return device(where["x"], where["y"], where["z"], core)

    barrier = pltpu.get_barrier_semaphore()
    waits = 0
    for axis in ("x", "y", "z"):
        for step in range(1, SIZES[axis]):
            pl.semaphore_signal(barrier, inc=1, device_id=peer(axis, step), device_id_type=MESH)
            waits += 1
    other_core = device(at["x"], at["y"], at["z"], 1 - core)
    pl.semaphore_signal(barrier, inc=1, device_id=other_core, device_id_type=MESH)
    waits += 1
    n_dom = NX * NZ * NCORE
    for off in OFFSETS:
        pl.semaphore_signal(barrier, inc=1, device_id=((dom + off + n_dom) % n_dom, sub), device_id_type=MESH)
        waits += 1

    base = sub * PAIRS
    for j in range(PAIRS):
        own[j, 0:3, :] = pos_ref[:, j * 128:(j + 1) * 128]
        own[j, 3:4, :] = mass_ref[j:j + 1, :]
    leaf_ref[pl.ds(base, PAIRS)] = own[...]
    pad[...] = jnp.zeros((128, 128), F32)
    pad[0:1, :] = cmass_ref[...]
    pad[1:4, :] = ccen_ref[...]
    pad[4:10, :] = cquad_ref[...]
    by_cell = pad[...].T
    packed = by_cell[0:16, :]
    for g in range(1, 8):
        packed = packed + pltpu.roll(by_cell[16 * g:16 * g + 16, :], 16 * g, 1)
    pad[0:16, :] = packed

    def start_of(part, done):
        first, rows, order = PARTS[part]
        size = rows
        n = N_CELL_ROWS // ROWS
        index = 0
        stride = 1
        for s, axis in enumerate(order):
            if s >= done:
                index = index + at[axis] * stride
            stride = stride * SIZES[axis]
        if done <= 3:
            index = index + core * stride
        for axis in order[:done]:
            size = size * SIZES[axis]
        return n * first + index * rows, size

    for part, (first, rows, order) in enumerate(PARTS):
        start, _ = start_of(part, 0)
        for r in range(rows):
            table_ref[start + r, :, :] = pad[first + r:first + r + 1, :]

    pl.semaphore_wait(barrier, waits)

    def cell_copy(part, stage, step):
        axis = PARTS[part][2][stage]
        start, size = start_of(part, stage)
        block = table_ref.at[pl.ds(start, size)]
        return pltpu.make_async_remote_copy(
            src_ref=block, dst_ref=block,
            send_sem=cell_send.at[part, stage, step], recv_sem=cell_recv.at[part, stage, step],
            device_id=peer(axis, step), device_id_type=MESH)

    def stage_copies(part, stage):
        return [cell_copy(part, stage, step) for step in range(1, SIZES[PARTS[part][2][stage]])]

    def core_copy(part):
        start, size = start_of(part, 3)
        block = table_ref.at[pl.ds(start, size)]
        return pltpu.make_async_remote_copy(
            src_ref=block, dst_ref=block, send_sem=core_send.at[part], recv_sem=core_recv.at[part],
            device_id=other_core, device_id_type=MESH)

    copies = [[stage_copies(part, stage) for stage in range(3)] for part in range(3)]
    core_copies = [core_copy(part) for part in range(3)]
    for part in range(3):
        for copy in copies[part][0]:
            copy.start()

    near = [
        pltpu.make_async_remote_copy(
            src_ref=own, dst_ref=leaf_ref.at[pl.ds(base, PAIRS)], send_sem=near_send.at[step], recv_sem=near_recv.at[step],
            device_id=peer("y", step), device_id_type=MESH)
        for step in range(1, NY)
    ]
    for copy in near:
        copy.start()

    low_half = lax.broadcasted_iota(jnp.int32, (4, 128), 1) < LEAF

    def far_pair(slot, t):
        halves = []
        for h in range(2):
            block = send_list[slot, 2 * t + h]
            tile = own[block // 2]
            turned = pltpu.roll(tile, LEAF, 1)
            picked = jnp.where(block % 2 == h, tile, turned)
            inside = jnp.logical_and(dom + OFFSETS[slot] >= 0, dom + OFFSETS[slot] < n_dom)
            live = jnp.logical_and(inside, 2 * t + h < send_count[slot])
            halves.append(jnp.where(live, picked, jnp.zeros_like(picked)))
        far_out[slot, t] = jnp.where(low_half, halves[0], halves[1])

    for slot in range(len(OFFSETS)):
        for t in range(CAP // 2):
            far_pair(slot, t)

    def far_copy(slot):
        return pltpu.make_async_remote_copy(
            src_ref=far_out.at[slot],
            dst_ref=leaf_ref.at[pl.ds(NY * PAIRS + slot * (CAP // 2), CAP // 2)],
            send_sem=far_send.at[slot], recv_sem=far_recv.at[slot],
            device_id=((dom + OFFSETS[slot] + n_dom) % n_dom, sub), device_id_type=MESH)

    far = [far_copy(slot) for slot in range(len(OFFSETS))]
    for copy in far:
        copy.start()

    for stage in range(3):
        for part in range(3):
            for copy in copies[part][stage]:
                copy.wait_recv()
            if stage < 2:
                for copy in copies[part][stage + 1]:
                    copy.start()
            else:
                core_copies[part].start()
    for copy in near:
        copy.wait()
    for copy in far:
        copy.wait()
    for part in range(3):
        for stage in range(3):
            for copy in copies[part][stage]:
                copy.wait_send()
        core_copies[part].wait()


def exchange(positions, masses, cell_mass, cell_center, cell_quad, send_list, send_count):
    vmem = pl.BlockSpec(memory_space=pltpu.VMEM)
    smem = pl.BlockSpec(memory_space=pltpu.SMEM)
    dma = pltpu.SemaphoreType.DMA
    return pl.pallas_call(
        exchange_kernel,
        name="exchange",
        out_shape=(
            jax.ShapeDtypeStruct((ALL_PAIRS, 4, 128), F32),
            jax.ShapeDtypeStruct((N_CELL_ROWS, 1, 128), F32),
        ),
        in_specs=[vmem] * 5 + [smem] * 2,
        out_specs=(vmem, vmem),
        scratch_shapes=[
            pltpu.VMEM((128, 128), F32),
            pltpu.VMEM((PAIRS, 4, 128), F32),
            pltpu.VMEM((len(OFFSETS), CAP // 2, 4, 128), F32),
            dma((NY,)), dma((NY,)), dma((len(OFFSETS),)), dma((len(OFFSETS),)),
            dma((3, 3, NZ)), dma((3, 3, NZ)), dma((3,)), dma((3,)),
        ],
        compiler_params=pltpu.CompilerParams(
            collective_id=0, has_side_effects=True, vmem_limit_bytes=24 * 1024 * 1024),
    )(positions, masses, cell_mass, cell_center, cell_quad, send_list, send_count)


def split3(value):
    high = value.astype(BF16).astype(F32)
    rest = value - high
    mid = rest.astype(BF16).astype(F32)
    return high, mid, rest - mid


def split2(value):
    high = value.astype(BF16)
    return high, (value - high.astype(F32)).astype(BF16)


def nt(a, b):
    return lax.dot_general(a, b, (((1,), (1,)), ((), ())), preferred_element_type=F32)


def cell_row(cell):
    shard = cell // 128
    sub = shard % NY
    dom = shard // NY
    at = {"x": dom // (NZ * NCORE), "z": (dom // NCORE) % NZ, "y": sub}
    core = dom % NCORE
    row = cell % 16
    n = N_CELL_ROWS // ROWS
    result = None
    for first, rows, order in PARTS:
        index, stride = 0, 1
        for axis in order:
            index = index + at[axis] * stride
            stride = stride * SIZES[axis]
        index = index + core * stride
        here = n * first + index * rows + (row - first)
        result = here if result is None else jnp.where(row >= first, here, result)
    return result


def pull_kernel(
    pos_ref, cells_ref, leaf_ids, leaf_ref, table_ref, out_ref,
    sources, targets, columns, rows_vmem, rows_smem, picked, row_sem,
):
    rows_vmem[...] = cell_row(cells_ref[...])
    row_copy = pltpu.make_async_copy(rows_vmem, rows_smem, row_sem)
    row_copy.start()

    row8 = lax.broadcasted_iota(jnp.int32, (8, 128), 0)
    one_row = jnp.where(row8 == 4, 1.0, 0.0).astype(F32)

    def prepare(pair, _):
        raw4 = leaf_ref[pair]
        raw = jnp.concatenate([raw4, raw4], axis=0)
        mass = raw4[3:4, :]
        centred = raw - 0.5
        square = jnp.where(row8 < 3, centred * centred, 0.0)
        norm = jnp.sum(square, axis=0, keepdims=True) + EPS
        u = jnp.where(row8 < 3, centred, jnp.where(row8 == 3, norm, one_row))
        s = jnp.where(row8 < 3, centred * mass, jnp.where(row8 == 3, mass, 0.0))
        u_high, u_mid, u_low = split3(u)
        s_high, s_mid, s_low = split3(s)
        s_top = s_high + pltpu.roll(s_mid, 4, 0)
        full = jnp.concatenate([u_high, u_mid, u_high, u_low, s_top, s_low], axis=0)
        sources[2 * pair] = full.astype(BF16)
        sources[2 * pair + 1] = pltpu.roll(full, LEAF, 1).astype(BF16)
        return 0

    lax.fori_loop(0, ALL_PAIRS, prepare, 0, unroll=4)

    for pair in range(PAIRS):
        raw3 = pos_ref[:, pair * 128:(pair + 1) * 128]
        raw = jnp.concatenate([raw3, jnp.zeros((5, 128), F32)], axis=0)
        centred = raw - 0.5
        square = jnp.where(row8 < 3, centred * centred, 0.0)
        norm = jnp.sum(square, axis=0, keepdims=True)
        t = jnp.where(row8 < 3, -2.0 * centred,
                      jnp.where(row8 == 3, 1.0, jnp.where(row8 == 4, norm, 0.0)))
        t_high, t_mid, t_low = split3(t)
        full = jnp.concatenate(
            [t_high, t_high, t_mid, t_mid, t_low, t_high, raw, jnp.zeros((128 - 56, 128), F32)], axis=0)
        turned = full.T
        targets[pair] = turned[:, 0:48].astype(BF16)
        columns[pair] = turned[:, 48:56]

    row_copy.wait()

    low_half = lax.broadcasted_iota(jnp.int32, (48, 128), 1) < LEAF
    summing_row = lax.broadcasted_iota(jnp.int32, (8, 768), 0)
    summing_lane = lax.broadcasted_iota(jnp.int32, (8, 768), 1)
    summing = jnp.where(summing_row == (summing_lane // 256), 1.0, 0.0).astype(BF16)

    def one_pair(pair, _):
        results = []
        centre = pos_ref[:, pl.ds(pl.multiple_of(pair * 128, 128), 128)] - 0.5
        for half in range(2):
            group = 2 * pair + half
            for k in range(NCELL):
                picked[half, k:k + 1, :] = table_ref[rows_smem[group, k]]
            lhs = targets[pair, half * 64:half * 64 + 64, :]
            total = None
            for tile in range(4):
                parts = []
                for j in range(2):
                    slot = 4 * tile + 2 * j
                    low = leaf_ids[slot, group]
                    high = leaf_ids[slot + 1, group]
                    parts.append(jnp.where(low_half, sources[low], sources[high ^ 1]))
                both = jnp.concatenate(parts, axis=1)
                rhs = jnp.concatenate([both[0:16], both[0:16], both[16:32]], axis=0)
                dist = jnp.dot(lhs, rhs, preferred_element_type=F32)
                inv = lax.rsqrt(dist)
                w_high, w_low = split2(inv * inv * inv)
                s = both[32:48]
                term = nt(s, w_high) + nt(s, w_low)
                total = term if total is None else total + term
            total = total[0:8] + total[8:16] + pltpu.roll(total[0:8], 4, 0)

            turned = picked[half].T
            lane_group = (cells_ref[pl.ds(group, 1), :] // 16) % 8
            feat = turned[0:16]
            for j in range(1, 8):
                feat = jnp.where(lane_group == j, turned[16 * j:16 * j + 16], feat)
            xyz = columns[pair, half * 64:half * 64 + 64, :]
            dx = xyz[:, 0:1] - feat[1:2]
            dy = xyz[:, 1:2] - feat[2:3]
            dz = xyz[:, 2:3] - feat[3:4]
            h = dx * dx + dy * dy + dz * dz + EPS
            inv = lax.rsqrt(h)
            inv2 = inv * inv
            inv3 = inv * inv2
            inv5 = inv3 * inv2
            qx = feat[4:5] * dx + feat[7:8] * dy + feat[8:9] * dz
            qy = feat[7:8] * dx + feat[5:6] * dy + feat[9:10] * dz
            qz = feat[8:9] * dx + feat[9:10] * dy + feat[6:7] * dz
            form = dx * qx + dy * qy + dz * qz
            along = feat[0:1] * inv3 + (2.5 * form) * (inv5 * inv2)
            pieces = []
            for d, q in ((dx, qx), (dy, qy), (dz, qz)):
                pieces.extend(split2(inv5 * q - along * d))
            far = nt(summing, jnp.concatenate(pieces, axis=1))
            here = total[0:3] - centre[:, half * 64:half * 64 + 64] * total[3:4]
            results.append(here + far[0:3])
        out_ref[:, pl.ds(pl.multiple_of(pair * 128, 128), 128)] = jnp.concatenate(results, axis=1)
        return 0

    lax.fori_loop(0, PAIRS, one_pair, 0)


def pull(positions, cell_list, leaf_list, leaves, table):
    vmem = pl.BlockSpec(memory_space=pltpu.VMEM)
    smem = pl.BlockSpec(memory_space=pltpu.SMEM)
    return pl.pallas_call(
        pull_kernel,
        name="pull",
        out_shape=jax.ShapeDtypeStruct((3, PAIRS * 128), F32),
        in_specs=[vmem, vmem, smem, vmem, vmem],
        out_specs=vmem,
        scratch_shapes=[
            pltpu.VMEM((2 * ALL_PAIRS, 48, 128), BF16),
            pltpu.VMEM((PAIRS, 128, 48), BF16),
            pltpu.VMEM((PAIRS, 128, 8), F32),
            pltpu.VMEM((128, 128), jnp.int32),
            pltpu.SMEM((128, 128), jnp.int32),
            pltpu.VMEM((2, 128, 128), F32),
            pltpu.SemaphoreType.DMA,
        ],
        compiler_params=pltpu.CompilerParams(vmem_limit_bytes=48 * 1024 * 1024),
    )(positions, cell_list, leaf_list, leaves, table)


def on_device(
    positions, masses, cell_mass, cell_center, cell_quad, cell_list, leaf_list, send_list, send_count,
):
    leaves, table = exchange(
        positions, masses.reshape(PAIRS, 128), cell_mass.reshape(1, 128), cell_center, cell_quad,
        send_list.reshape(2 * RANGE, CAP), send_count.reshape(2 * RANGE))
    return pull(positions, cell_list, leaf_list.T, leaves, table)


def solution(mesh):
    return jax.shard_map(
        on_device,
        mesh=mesh,
        in_specs=(
            P(None, ("dom", "sub")),
            P(("dom", "sub")),
            P(("dom", "sub")),
            P(None, ("dom", "sub")),
            P(None, ("dom", "sub")),
            P(("dom", "sub"), None),
            P(("dom", "sub"), None),
            P("dom", "sub", None, None),
            P("dom", "sub", None),
        ),
        out_specs=P(None, ("dom", "sub")),
        check_vma=False,
    )
```

```python
import functools

import jax
import jax.numpy as jnp
from jax import lax
from jax.experimental import pallas as pl
from jax.experimental.pallas import tpu as pltpu
from jax.sharding import PartitionSpec as P

LEAF = 64
NCELL = 128
NLEAF = 16
RANGE = 4
CAP = 8
EPS = 0.0025
F32 = jnp.float32
BF16 = jnp.bfloat16
MESH = pl.DeviceIdType.MESH

NX, NY, NZ, NCORE = 4, 4, 8, 2
SIZES = {"x": NX, "y": NY, "z": NZ}
ROWS = 16
PARTS = ((0, 6, ("z", "x", "y")), (6, 5, ("x", "y", "z")), (11, 5, ("y", "z", "x")))
OFFSETS = tuple(range(-RANGE, 0)) + tuple(range(1, RANGE + 1))
PAIRS = 64
ALL_PAIRS = NY * PAIRS + len(OFFSETS) * CAP // 2
N_CELL_ROWS = NX * NY * NZ * NCORE * ROWS


def exchange_kernel(
    pos_ref, mass_ref, cmass_ref, ccen_ref, cquad_ref, send_list, send_count,
    leaf_ref, table_ref,
    pad, own, far_out, near_send, near_recv, far_send, far_recv, cell_send, cell_recv, core_send, core_recv,
):
    dom = lax.axis_index("dom")
    sub = lax.axis_index("sub")
    core = dom % NCORE
    at = {"x": dom // (NZ * NCORE), "z": (dom // NCORE) % NZ, "y": sub}

    def device(x, y, z, c):
        return ((x * NZ + z) * NCORE + c, y)

    def peer(axis, step):
        where = dict(at)
        where[axis] = (at[axis] + step) % SIZES[axis]
        return device(where["x"], where["y"], where["z"], core)

    barrier = pltpu.get_barrier_semaphore()
    waits = 0
    for axis in ("x", "y", "z"):
        for step in range(1, SIZES[axis]):
            pl.semaphore_signal(barrier, inc=1, device_id=peer(axis, step), device_id_type=MESH)
            waits += 1
    other_core = device(at["x"], at["y"], at["z"], 1 - core)
    pl.semaphore_signal(barrier, inc=1, device_id=other_core, device_id_type=MESH)
    waits += 1
    n_dom = NX * NZ * NCORE
    for off in OFFSETS:
        pl.semaphore_signal(barrier, inc=1, device_id=((dom + off + n_dom) % n_dom, sub), device_id_type=MESH)
        waits += 1

    base = sub * PAIRS
    for j in range(PAIRS):
        own[j, 0:3, :] = pos_ref[:, j * 128:(j + 1) * 128]
        own[j, 3:4, :] = mass_ref[j:j + 1, :]
    leaf_ref[pl.ds(base, PAIRS)] = own[...]
    pad[...] = jnp.zeros((128, 128), F32)
    pad[0:1, :] = cmass_ref[...]
    pad[1:4, :] = ccen_ref[...]
    pad[4:10, :] = cquad_ref[...]
    by_cell = pad[...].T
    packed = by_cell[0:16, :]
    for g in range(1, 8):
        packed = packed + pltpu.roll(by_cell[16 * g:16 * g + 16, :], 16 * g, 1)
    pad[0:16, :] = packed

    def start_of(part, done):
        first, rows, order = PARTS[part]
        size = rows
        n = N_CELL_ROWS // ROWS
        index = 0
        stride = 1
        for s, axis in enumerate(order):
            if s >= done:
                index = index + at[axis] * stride
            stride = stride * SIZES[axis]
        if done <= 3:
            index = index + core * stride
        for axis in order[:done]:
            size = size * SIZES[axis]
        return n * first + index * rows, size

    for part, (first, rows, order) in enumerate(PARTS):
        start, _ = start_of(part, 0)
        for r in range(rows):
            table_ref[start + r, :, :] = pad[first + r:first + r + 1, :]

    pl.semaphore_wait(barrier, waits)

    def cell_copy(part, stage, step):
        axis = PARTS[part][2][stage]
        start, size = start_of(part, stage)
        block = table_ref.at[pl.ds(start, size)]
        return pltpu.make_async_remote_copy(
            src_ref=block, dst_ref=block,
            send_sem=cell_send.at[part, stage, step], recv_sem=cell_recv.at[part, stage, step],
            device_id=peer(axis, step), device_id_type=MESH)

    def stage_copies(part, stage):
        return [cell_copy(part, stage, step) for step in range(1, SIZES[PARTS[part][2][stage]])]

    def core_copy(part):
        start, size = start_of(part, 3)
        block = table_ref.at[pl.ds(start, size)]
        return pltpu.make_async_remote_copy(
            src_ref=block, dst_ref=block, send_sem=core_send.at[part], recv_sem=core_recv.at[part],
            device_id=other_core, device_id_type=MESH)

    copies = [[stage_copies(part, stage) for stage in range(3)] for part in range(3)]
    core_copies = [core_copy(part) for part in range(3)]
    for part in range(3):
        for copy in copies[part][0]:
            copy.start()

    near = [
        pltpu.make_async_remote_copy(
            src_ref=own, dst_ref=leaf_ref.at[pl.ds(base, PAIRS)], send_sem=near_send.at[step], recv_sem=near_recv.at[step],
            device_id=peer("y", step), device_id_type=MESH)
        for step in range(1, NY)
    ]
    for copy in near:
        copy.start()

    low_half = lax.broadcasted_iota(jnp.int32, (4, 128), 1) < LEAF

    def far_pair(slot, t):
        halves = []
        for h in range(2):
            block = send_list[slot, 2 * t + h]
            tile = own[block // 2]
            turned = pltpu.roll(tile, LEAF, 1)
            picked = jnp.where(block % 2 == h, tile, turned)
            inside = jnp.logical_and(dom + OFFSETS[slot] >= 0, dom + OFFSETS[slot] < n_dom)
            live = jnp.logical_and(inside, 2 * t + h < send_count[slot])
            halves.append(jnp.where(live, picked, jnp.zeros_like(picked)))
        far_out[slot, t] = jnp.where(low_half, halves[0], halves[1])

    for slot in range(len(OFFSETS)):
        for t in range(CAP // 2):
            far_pair(slot, t)

    def far_copy(slot):
        return pltpu.make_async_remote_copy(
            src_ref=far_out.at[slot],
            dst_ref=leaf_ref.at[pl.ds(NY * PAIRS + slot * (CAP // 2), CAP // 2)],
            send_sem=far_send.at[slot], recv_sem=far_recv.at[slot],
            device_id=((dom + OFFSETS[slot] + n_dom) % n_dom, sub), device_id_type=MESH)

    far = [far_copy(slot) for slot in range(len(OFFSETS))]
    for copy in far:
        copy.start()

    for stage in range(3):
        for part in range(3):
            for copy in copies[part][stage]:
                copy.wait_recv()
            if stage < 2:
                for copy in copies[part][stage + 1]:
                    copy.start()
            else:
                core_copies[part].start()
    for copy in near:
        copy.wait()
    for copy in far:
        copy.wait()
    for part in range(3):
        for stage in range(3):
            for copy in copies[part][stage]:
                copy.wait_send()
        core_copies[part].wait()


def exchange(positions, masses, cell_mass, cell_center, cell_quad, send_list, send_count):
    vmem = pl.BlockSpec(memory_space=pltpu.VMEM)
    smem = pl.BlockSpec(memory_space=pltpu.SMEM)
    dma = pltpu.SemaphoreType.DMA
    return pl.pallas_call(
        exchange_kernel,
        name="exchange",
        out_shape=(
            jax.ShapeDtypeStruct((ALL_PAIRS, 4, 128), F32),
            jax.ShapeDtypeStruct((N_CELL_ROWS, 1, 128), F32),
        ),
        in_specs=[vmem] * 5 + [smem] * 2,
        out_specs=(vmem, vmem),
        scratch_shapes=[
            pltpu.VMEM((128, 128), F32),
            pltpu.VMEM((PAIRS, 4, 128), F32),
            pltpu.VMEM((len(OFFSETS), CAP // 2, 4, 128), F32),
            dma((NY,)), dma((NY,)), dma((len(OFFSETS),)), dma((len(OFFSETS),)),
            dma((3, 3, NZ)), dma((3, 3, NZ)), dma((3,)), dma((3,)),
        ],
        compiler_params=pltpu.CompilerParams(
            collective_id=0, has_side_effects=True, vmem_limit_bytes=24 * 1024 * 1024),
    )(positions, masses, cell_mass, cell_center, cell_quad, send_list, send_count)


def split3(value):
    high = value.astype(BF16).astype(F32)
    rest = value - high
    mid = rest.astype(BF16).astype(F32)
    return high, mid, rest - mid


def split2(value):
    high = value.astype(BF16)
    return high, (value - high.astype(F32)).astype(BF16)


def nt(a, b):
    return lax.dot_general(a, b, (((1,), (1,)), ((), ())), preferred_element_type=F32)


def cell_row(cell):
    shard = cell // 128
    sub = shard % NY
    dom = shard // NY
    at = {"x": dom // (NZ * NCORE), "z": (dom // NCORE) % NZ, "y": sub}
    core = dom % NCORE
    row = cell % 16
    n = N_CELL_ROWS // ROWS
    result = None
    for first, rows, order in PARTS:
        index, stride = 0, 1
        for axis in order:
            index = index + at[axis] * stride
            stride = stride * SIZES[axis]
        index = index + core * stride
        here = n * first + index * rows + (row - first)
        result = here if result is None else jnp.where(row >= first, here, result)
    return result


def pull_kernel(
    pos_ref, cells_ref, leaf_ids, leaf_ref, table_ref, out_ref,
    features, moments, targets, columns, rows_vmem, rows_smem, picked_a, picked_b, dist_a, dist_b, row_sem,
):
    rows_vmem[...] = cell_row(cells_ref[...])
    row_copy = pltpu.make_async_copy(rows_vmem, rows_smem, row_sem)
    row_copy.start()

    row8 = lax.broadcasted_iota(jnp.int32, (8, 128), 0)
    one_row = jnp.where(row8 == 4, 1.0, 0.0).astype(F32)
    no_rows = jnp.zeros((16, 128), F32)

    def prepare(pair, _):
        raw4 = leaf_ref[pair]
        raw = jnp.concatenate([raw4, raw4], axis=0)
        mass = raw4[3:4, :]
        centred = raw - 0.5
        square = jnp.where(row8 < 3, centred * centred, 0.0)
        norm = jnp.sum(square, axis=0, keepdims=True) + EPS
        u = jnp.where(row8 < 3, centred, jnp.where(row8 == 3, norm, one_row))
        s = jnp.where(row8 < 3, centred * mass, jnp.where(row8 == 3, mass, 0.0))
        u_high, u_mid, u_low = split3(u)
        s_high, s_mid, s_low = split3(s)
        s_full = jnp.concatenate([s_high + pltpu.roll(s_mid, 4, 0), s_low], axis=0)
        moments[2 * pair] = s_full.astype(BF16)
        moments[2 * pair + 1] = pltpu.roll(s_full, LEAF, 1).astype(BF16)
        u_full = jnp.concatenate([u_high, u_mid, u_high, u_mid, u_high, u_low, no_rows], axis=0).astype(BF16)
        turned = jnp.concatenate([u_full, u_full], axis=0).T
        features[2 * pair] = turned[0:64]
        features[2 * pair + 1] = turned[64:128]
        return 0

    lax.fori_loop(0, ALL_PAIRS, prepare, 0, unroll=4)

    def prepare_targets(pair, _):
        raw3 = pos_ref[:, pl.ds(pl.multiple_of(pair * 128, 128), 128)]
        raw = jnp.concatenate([raw3, jnp.zeros((5, 128), F32)], axis=0)
        centred = raw - 0.5
        square = jnp.where(row8 < 3, centred * centred, 0.0)
        norm = jnp.sum(square, axis=0, keepdims=True)
        t = jnp.where(row8 < 3, -2.0 * centred,
                      jnp.where(row8 == 3, 1.0, jnp.where(row8 == 4, norm, 0.0)))
        t_high, t_mid, t_low = split3(t)
        targets[pair] = jnp.concatenate(
            [t_high, t_high, t_mid, t_mid, t_low, t_high, no_rows], axis=0).astype(BF16)
        columns[pair] = jnp.concatenate([raw, jnp.zeros((120, 128), F32)], axis=0).T[:, 0:8]
        return 0

    lax.fori_loop(0, PAIRS, prepare_targets, 0, unroll=4)
    row_copy.wait()

    low_half = lax.broadcasted_iota(jnp.int32, (64, 128), 1) < LEAF
    low_half16 = lax.broadcasted_iota(jnp.int32, (16, 128), 1) < LEAF
    summing_row = lax.broadcasted_iota(jnp.int32, (8, 768), 0)
    summing_lane = lax.broadcasted_iota(jnp.int32, (8, 768), 1)
    summing = jnp.where(summing_row == (summing_lane // 256), 1.0, 0.0).astype(BF16)
    lane_block = lax.broadcasted_iota(jnp.int32, (8, 256), 1) // LEAF
    nothing = jnp.zeros((64, 128), BF16)

    def target_weights(quad):
        blocks = []
        for half in range(2):
            tile = targets[2 * quad + half]
            own = jnp.concatenate(
                [jnp.where(low_half, tile, nothing), jnp.where(low_half, nothing, tile)], axis=0)
            empty = jnp.zeros((128, 128), BF16)
            blocks.append(jnp.concatenate([own, empty] if half == 0 else [empty, own], axis=0))
        return jnp.concatenate(blocks, axis=1)

    def fetch(quad, part, weights, picked, dist):
        group = 4 * quad + part
        for k in range(NCELL):
            picked[part, k:k + 1, :] = table_ref[rows_smem[group, k]]
        rows = []
        for slot in range(4 * part, 4 * part + 4):
            halves = []
            for half in range(2):
                first = leaf_ids[slot, 4 * quad + 2 * half]
                second = leaf_ids[slot, 4 * quad + 2 * half + 1]
                halves.append(jnp.where(low_half, features[first], features[second]))
            rows.append(jnp.concatenate(halves, axis=1))
        lhs = jnp.concatenate(rows, axis=0)
        dist[part] = jnp.dot(lhs, weights, preferred_element_type=F32)

    def weigh(quad, part, dist, totals):
        inv = lax.rsqrt(dist[part])
        w_high, w_low = split2(inv * inv * inv)
        rows = []
        for j in range(4):
            group = 4 * quad + j
            tiles = []
            for slot in range(4 * part, 4 * part + 4, 2):
                low = leaf_ids[slot, group]
                high = leaf_ids[slot + 1, group]
                tiles.append(jnp.where(low_half16, moments[low], moments[high ^ 1]))
            rows.append(jnp.concatenate(tiles, axis=1))
        full = jnp.concatenate(rows, axis=0)
        short = jnp.concatenate([row[0:8] for row in rows], axis=0)
        high = jnp.dot(full, w_high, preferred_element_type=F32)
        low = jnp.dot(short, w_low, preferred_element_type=F32)
        if totals is None:
            return high, low
        return totals[0] + high, totals[1] + low

    def multipole(quad, part, picked):
        group = 4 * quad + part
        turned = picked[part].T
        lane_group = (cells_ref[pl.ds(group, 1), :] // 16) % 8
        feat = turned[0:16]
        for j in range(1, 8):
            feat = jnp.where(lane_group == j, turned[16 * j:16 * j + 16], feat)
        xyz = columns[2 * quad + part // 2, (part % 2) * 64:(part % 2) * 64 + 64, :]
        dx = xyz[:, 0:1] - feat[1:2]
        dy = xyz[:, 1:2] - feat[2:3]
        dz = xyz[:, 2:3] - feat[3:4]
        h = dx * dx + dy * dy + dz * dz + EPS
        inv = lax.rsqrt(h)
        inv2 = inv * inv
        inv3 = inv * inv2
        inv5 = inv3 * inv2
        qx = feat[4:5] * dx + feat[7:8] * dy + feat[8:9] * dz
        qy = feat[7:8] * dx + feat[5:6] * dy + feat[9:10] * dz
        qz = feat[8:9] * dx + feat[9:10] * dy + feat[6:7] * dz
        form = dx * qx + dy * qy + dz * qz
        along = feat[0:1] * inv3 + (2.5 * form) * (inv5 * inv2)
        pieces = []
        for d, q in ((dx, qx), (dy, qy), (dz, qz)):
            pieces.extend(split2(inv5 * q - along * d))
        return jnp.concatenate(pieces, axis=1)

    def step(quad, picked, dist, later, later_picked, later_dist):
        totals = None
        pieces = []
        weights = target_weights(later)
        for part in range(4):
            fetch(later, part, weights, later_picked, later_dist)
            totals = weigh(quad, part, dist, totals)
            pieces.append(multipole(quad, part, picked))
        far = nt(summing, jnp.concatenate(pieces, axis=0))
        high, low = totals
        near = jnp.zeros((8, 256), F32)
        for j in range(4):
            block = high[16 * j:16 * j + 8] + high[16 * j + 8:16 * j + 16] + low[8 * j:8 * j + 8]
            near = jnp.where(lane_block == j, block, near)
        near = near + pltpu.roll(near, 4, 0)
        lanes = pl.ds(pl.multiple_of(quad * 256, 256), 256)
        centre = pos_ref[:, lanes] - 0.5
        out_ref[:, lanes] = near[0:3] - centre * near[3:4] + far[0:3]

    first_weights = target_weights(0)
    for part in range(4):
        fetch(0, part, first_weights, picked_a, dist_a)
    quads = PAIRS // 2

    def two_quads(i, _):
        step(2 * i, picked_a, dist_a, 2 * i + 1, picked_b, dist_b)
        step(2 * i + 1, picked_b, dist_b, jnp.minimum(2 * i + 2, quads - 1), picked_a, dist_a)
        return 0

    lax.fori_loop(0, quads // 2, two_quads, 0)


def pull(positions, cell_list, leaf_list, leaves, table):
    vmem = pl.BlockSpec(memory_space=pltpu.VMEM)
    smem = pl.BlockSpec(memory_space=pltpu.SMEM)
    return pl.pallas_call(
        pull_kernel,
        name="pull",
        out_shape=jax.ShapeDtypeStruct((3, PAIRS * 128), F32),
        in_specs=[vmem, vmem, smem, vmem, vmem],
        out_specs=vmem,
        scratch_shapes=[
            pltpu.VMEM((2 * ALL_PAIRS, 64, 128), BF16),
            pltpu.VMEM((2 * ALL_PAIRS, 16, 128), BF16),
            pltpu.VMEM((PAIRS, 64, 128), BF16),
            pltpu.VMEM((PAIRS, 128, 8), F32),
            pltpu.VMEM((128, 128), jnp.int32),
            pltpu.SMEM((128, 128), jnp.int32),
            pltpu.VMEM((4, 128, 128), F32),
            pltpu.VMEM((4, 128, 128), F32),
            pltpu.VMEM((4, 256, 256), F32),
            pltpu.VMEM((4, 256, 256), F32),
            pltpu.SemaphoreType.DMA,
        ],
        compiler_params=pltpu.CompilerParams(vmem_limit_bytes=48 * 1024 * 1024),
    )(positions, cell_list, leaf_list, leaves, table)


def on_device(
    positions, masses, cell_mass, cell_center, cell_quad, cell_list, leaf_list, send_list, send_count,
):
    leaves, table = exchange(
        positions, masses.reshape(PAIRS, 128), cell_mass.reshape(1, 128), cell_center, cell_quad,
        send_list.reshape(2 * RANGE, CAP), send_count.reshape(2 * RANGE))
    return pull(positions, cell_list, leaf_list.T, leaves, table)


def solution(mesh):
    return jax.shard_map(
        on_device,
        mesh=mesh,
        in_specs=(
            P(None, ("dom", "sub")),
            P(("dom", "sub")),
            P(("dom", "sub")),
            P(None, ("dom", "sub")),
            P(None, ("dom", "sub")),
            P(("dom", "sub"), None),
            P(("dom", "sub"), None),
            P("dom", "sub", None, None),
            P("dom", "sub", None),
        ),
        out_specs=P(None, ("dom", "sub")),
        check_vma=False,
    )
```

```python
import functools

import jax
import jax.numpy as jnp
from jax import lax
from jax.experimental import pallas as pl
from jax.experimental.pallas import tpu as pltpu
from jax.sharding import PartitionSpec as P

LEAF = 64
NCELL = 128
NLEAF = 16
RANGE = 4
CAP = 8
EPS = 0.0025
F32 = jnp.float32
BF16 = jnp.bfloat16
MESH = pl.DeviceIdType.MESH

NX, NY, NZ, NCORE = 4, 4, 8, 2
SIZES = {"x": NX, "y": NY, "z": NZ}
ROWS = 16
PARTS = ((0, 8, ("z", "x", "y")), (8, 8, ("z", "y", "x")))
OFFSETS = tuple(range(-RANGE, 0)) + tuple(range(1, RANGE + 1))
PAIRS = 64
ALL_PAIRS = NY * PAIRS + len(OFFSETS) * CAP // 2
N_CELL_ROWS = NX * NY * NZ * NCORE * ROWS
STAGE_AT = ((0, 1), (8, 2))


def split3(value):
    high = value.astype(BF16).astype(F32)
    rest = value - high
    mid = rest.astype(BF16).astype(F32)
    return high, mid, rest - mid


def split2(value):
    high = value.astype(BF16)
    return high, (value - high.astype(F32)).astype(BF16)


def nt(a, b):
    return lax.dot_general(a, b, (((1,), (1,)), ((), ())), preferred_element_type=F32)


def cell_row(cell):
    shard = cell // 128
    sub = shard % NY
    dom = shard // NY
    at = {"x": dom // (NZ * NCORE), "z": (dom // NCORE) % NZ, "y": sub}
    core = dom % NCORE
    row = cell % 16
    n = N_CELL_ROWS // ROWS
    result = None
    for first, rows, order in PARTS:
        index, stride = 0, 1
        for axis in order:
            index = index + at[axis] * stride
            stride = stride * SIZES[axis]
        index = index + core * stride
        here = n * first + index * rows + (row - first)
        result = here if result is None else jnp.where(row >= first, here, result)
    return result


def kernel(
    pos_hbm, mass_hbm, cmass_hbm, ccen_hbm, cquad_hbm, cells_hbm, leaf_hbm, list_hbm, count_hbm,
    out_ref,
    pos_ref, mass_ref, cmass_ref, ccen_ref, cquad_ref, cells_ref, leaf_ids, send_list, send_count,
    pad, own, far_out, leaf_ref, table_ref,
    features, moments, targets, columns, rows_vmem, rows_smem, picked_a, picked_b, dist_a, dist_b,
    load_sem, row_sem, near_send, near_recv, far_send, far_recv, cell_send, cell_recv, core_send, core_recv,
):
    dom = lax.axis_index("dom")
    sub = lax.axis_index("sub")
    core = dom % NCORE
    at = {"x": dom // (NZ * NCORE), "z": (dom // NCORE) % NZ, "y": sub}
    n_dom = NX * NZ * NCORE
    base = sub * PAIRS

    loads = [
        pltpu.make_async_copy(src, dst, load_sem.at[i])
        for i, (src, dst) in enumerate((
            (pos_hbm, pos_ref), (mass_hbm, mass_ref), (cmass_hbm, cmass_ref), (ccen_hbm, ccen_ref),
            (cquad_hbm, cquad_ref), (list_hbm, send_list), (count_hbm, send_count), (cells_hbm, cells_ref),
            (leaf_hbm, leaf_ids)))
    ]
    for load in loads:
        load.start()

    def device(x, y, z, c):
        return ((x * NZ + z) * NCORE + c, y)

    def peer(axis, step):
        where = dict(at)
        where[axis] = (at[axis] + step) % SIZES[axis]
        return device(where["x"], where["y"], where["z"], core)

    barrier = pltpu.get_barrier_semaphore()
    waits = 0
    for axis in ("x", "y", "z"):
        for step in range(1, SIZES[axis]):
            pl.semaphore_signal(barrier, inc=1, device_id=peer(axis, step), device_id_type=MESH)
            waits += 1
    other_core = device(at["x"], at["y"], at["z"], 1 - core)
    pl.semaphore_signal(barrier, inc=1, device_id=other_core, device_id_type=MESH)
    waits += 1
    for off in OFFSETS:
        pl.semaphore_signal(barrier, inc=1, device_id=((dom + off + n_dom) % n_dom, sub), device_id_type=MESH)
        waits += 1

    for load in loads[0:5]:
        load.wait()
    for j in range(PAIRS):
        own[j, 0:3, :] = pos_ref[:, j * 128:(j + 1) * 128]
        own[j, 3:4, :] = mass_ref[j:j + 1, :]
    pad[...] = jnp.zeros((128, 128), F32)
    pad[0:1, :] = cmass_ref[...]
    pad[1:4, :] = ccen_ref[...]
    pad[4:10, :] = cquad_ref[...]
    by_cell = pad[...].T
    packed = by_cell[0:16, :]
    for g in range(1, 8):
        packed = packed + pltpu.roll(by_cell[16 * g:16 * g + 16, :], 16 * g, 1)
    pad[0:16, :] = packed

    def start_of(part, done):
        first, rows, order = PARTS[part]
        size = rows
        n = N_CELL_ROWS // ROWS
        index = 0
        stride = 1
        for s, axis in enumerate(order):
            if s >= done:
                index = index + at[axis] * stride
            stride = stride * SIZES[axis]
        index = index + core * stride
        for axis in order[:done]:
            size = size * SIZES[axis]
        return n * first + index * rows, size

    for part, (first, rows, order) in enumerate(PARTS):
        start, _ = start_of(part, 0)
        for r in range(rows):
            table_ref[start + r, :, :] = pad[first + r:first + r + 1, :]

    pl.semaphore_wait(barrier, waits)

    def cell_copy(part, stage, step):
        axis = PARTS[part][2][stage]
        start, size = start_of(part, stage)
        block = table_ref.at[pl.ds(start, size)]
        return pltpu.make_async_remote_copy(
            src_ref=block, dst_ref=block,
            send_sem=cell_send.at[part, stage, step], recv_sem=cell_recv.at[part, stage, step],
            device_id=peer(axis, step), device_id_type=MESH)

    def stage_copies(part, stage):
        return [cell_copy(part, stage, step) for step in range(1, SIZES[PARTS[part][2][stage]])]

    def core_copy(part):
        start, size = start_of(part, 3)
        block = table_ref.at[pl.ds(start, size)]
        return pltpu.make_async_remote_copy(
            src_ref=block, dst_ref=block, send_sem=core_send.at[part], recv_sem=core_recv.at[part],
            device_id=other_core, device_id_type=MESH)

    n_parts = len(PARTS)

    def start_stage(stage):
        for part in range(n_parts):
            if stage == 3:
                core_copy(part).start()
            else:
                for copy in stage_copies(part, stage):
                    copy.start()

    def finish_stage(stage):
        for part in range(n_parts):
            if stage == 3:
                core_copy(part).wait_recv()
            else:
                for copy in stage_copies(part, stage):
                    copy.wait_recv()

    near = [
        pltpu.make_async_remote_copy(
            src_ref=own, dst_ref=leaf_ref.at[pl.ds(base, PAIRS)],
            send_sem=near_send.at[step], recv_sem=near_recv.at[step],
            device_id=peer("y", step), device_id_type=MESH)
        for step in range(1, NY)
    ]
    for copy in near:
        copy.start()
    start_stage(0)

    for load in loads[5:7]:
        load.wait()
    low_half4 = lax.broadcasted_iota(jnp.int32, (4, 128), 1) < LEAF

    def far_pair(slot, t):
        halves = []
        for h in range(2):
            block = send_list[slot, 2 * t + h]
            tile = own[block // 2]
            turned = pltpu.roll(tile, LEAF, 1)
            picked = jnp.where(block % 2 == h, tile, turned)
            inside = jnp.logical_and(dom + OFFSETS[slot] >= 0, dom + OFFSETS[slot] < n_dom)
            live = jnp.logical_and(inside, 2 * t + h < send_count[slot])
            halves.append(jnp.where(live, picked, jnp.zeros_like(picked)))
        far_out[slot, t] = jnp.where(low_half4, halves[0], halves[1])

    def far_copy(slot):
        return pltpu.make_async_remote_copy(
            src_ref=far_out.at[slot],
            dst_ref=leaf_ref.at[pl.ds(NY * PAIRS + slot * (CAP // 2), CAP // 2)],
            send_sem=far_send.at[slot], recv_sem=far_recv.at[slot],
            device_id=((dom + OFFSETS[slot] + n_dom) % n_dom, sub), device_id_type=MESH)

    for slot in range(len(OFFSETS)):
        for t in range(CAP // 2):
            far_pair(slot, t)
    far = [far_copy(slot) for slot in range(len(OFFSETS))]
    for copy in far:
        copy.start()

    for load in loads[7:9]:
        load.wait()
    rows_vmem[...] = cell_row(cells_ref[...])
    row_copy = pltpu.make_async_copy(rows_vmem, rows_smem, row_sem)
    row_copy.start()

    row8 = lax.broadcasted_iota(jnp.int32, (8, 128), 0)
    one_row = jnp.where(row8 == 4, 1.0, 0.0).astype(F32)
    no_rows = jnp.zeros((16, 128), F32)

    def prepare(source_ref, source, pair):
        raw4 = source_ref[source]
        raw = jnp.concatenate([raw4, raw4], axis=0)
        mass = raw4[3:4, :]
        centred = raw - 0.5
        square = jnp.where(row8 < 3, centred * centred, 0.0)
        norm = jnp.sum(square, axis=0, keepdims=True) + EPS
        u = jnp.where(row8 < 3, centred, jnp.where(row8 == 3, norm, one_row))
        s = jnp.where(row8 < 3, centred * mass, jnp.where(row8 == 3, mass, 0.0))
        u_high, u_mid, u_low = split3(u)
        s_high, s_mid, s_low = split3(s)
        s_full = jnp.concatenate([s_high + pltpu.roll(s_mid, 4, 0), s_low], axis=0)
        moments[2 * pair] = s_full.astype(BF16)
        moments[2 * pair + 1] = pltpu.roll(s_full, LEAF, 1).astype(BF16)
        u_full = jnp.concatenate([u_high, u_mid, u_high, u_mid, u_high, u_low, no_rows], axis=0).astype(BF16)
        turned = jnp.concatenate([u_full, u_full], axis=0).T
        features[2 * pair] = turned[0:64]
        features[2 * pair + 1] = turned[64:128]

    def prepare_range(source_ref, source, pair, count):
        def body(j, _):
            prepare(source_ref, source + j, pair + j)
            return 0
        lax.fori_loop(0, count, body, 0, unroll=4)

    def prepare_targets(pair, _):
        raw3 = pos_ref[:, pl.ds(pl.multiple_of(pair * 128, 128), 128)]
        raw = jnp.concatenate([raw3, jnp.zeros((5, 128), F32)], axis=0)
        centred = raw - 0.5
        square = jnp.where(row8 < 3, centred * centred, 0.0)
        norm = jnp.sum(square, axis=0, keepdims=True)
        t = jnp.where(row8 < 3, -2.0 * centred,
                      jnp.where(row8 == 3, 1.0, jnp.where(row8 == 4, norm, 0.0)))
        t_high, t_mid, t_low = split3(t)
        targets[pair] = jnp.concatenate(
            [t_high, t_high, t_mid, t_mid, t_low, t_high, no_rows], axis=0).astype(BF16)
        columns[pair] = jnp.concatenate([raw, jnp.zeros((120, 128), F32)], axis=0).T[:, 0:8]
        return 0

    prepare_range(own, 0, base, PAIRS)
    lax.fori_loop(0, PAIRS, prepare_targets, 0, unroll=4)
    finish_stage(0)
    start_stage(1)
    for copy in far:
        copy.wait_recv()
    prepare_range(leaf_ref, NY * PAIRS, NY * PAIRS, len(OFFSETS) * CAP // 2)
    for step in range(1, NY):
        near[step - 1].wait_recv()
        origin = ((sub + NY - step) % NY) * PAIRS
        prepare_range(leaf_ref, origin, origin, PAIRS)

    low_half = lax.broadcasted_iota(jnp.int32, (64, 128), 1) < LEAF
    low_half16 = lax.broadcasted_iota(jnp.int32, (16, 128), 1) < LEAF
    summing_row = lax.broadcasted_iota(jnp.int32, (8, 768), 0)
    summing_lane = lax.broadcasted_iota(jnp.int32, (8, 768), 1)
    summing = jnp.where(summing_row == (summing_lane // 256), 1.0, 0.0).astype(BF16)
    lane_block = lax.broadcasted_iota(jnp.int32, (8, 256), 1) // LEAF
    nothing = jnp.zeros((64, 128), BF16)
    empty = jnp.zeros((128, 128), BF16)

    def target_weights(quad):
        blocks = []
        for half in range(2):
            tile = targets[2 * quad + half]
            diagonal = jnp.concatenate(
                [jnp.where(low_half, tile, nothing), jnp.where(low_half, nothing, tile)], axis=0)
            blocks.append(jnp.concatenate([diagonal, empty] if half == 0 else [empty, diagonal], axis=0))
        return jnp.concatenate(blocks, axis=1)

    def distances(quad, part, weights, dist):
        rows = []
        for slot in range(4 * part, 4 * part + 4):
            halves = []
            for half in range(2):
                first = leaf_ids[slot, 4 * quad + 2 * half]
                second = leaf_ids[slot, 4 * quad + 2 * half + 1]
                halves.append(jnp.where(low_half, features[first], features[second]))
            rows.append(jnp.concatenate(halves, axis=1))
        lhs = jnp.concatenate(rows, axis=0)
        dist[part] = jnp.dot(lhs, weights, preferred_element_type=F32)

    def weigh(quad, part, dist, totals):
        inv = lax.rsqrt(dist[part])
        w_high, w_low = split2(inv * inv * inv)
        rows = []
        for j in range(4):
            group = 4 * quad + j
            tiles = []
            for slot in range(4 * part, 4 * part + 4, 2):
                low = leaf_ids[slot, group]
                high = leaf_ids[slot + 1, group]
                tiles.append(jnp.where(low_half16, moments[low], moments[high ^ 1]))
            rows.append(jnp.concatenate(tiles, axis=1))
        full = jnp.concatenate(rows, axis=0)
        short = jnp.concatenate([row[0:8] for row in rows], axis=0)
        high = jnp.dot(full, w_high, preferred_element_type=F32)
        low = jnp.dot(short, w_low, preferred_element_type=F32)
        if totals is None:
            return high, low
        return totals[0] + high, totals[1] + low

    def quad_lanes(quad):
        return pl.ds(pl.multiple_of(quad * 256, 256), 256)

    def direct(quad, dist, later, later_dist):
        totals = None
        weights = target_weights(later)
        for part in range(4):
            distances(later, part, weights, later_dist)
            totals = weigh(quad, part, dist, totals)
        high, low = totals
        near_sum = jnp.zeros((8, 256), F32)
        for j in range(4):
            block = high[16 * j:16 * j + 8] + high[16 * j + 8:16 * j + 16] + low[8 * j:8 * j + 8]
            near_sum = jnp.where(lane_block == j, block, near_sum)
        near_sum = near_sum + pltpu.roll(near_sum, 4, 0)
        lanes = quad_lanes(quad)
        centre = pos_ref[:, lanes] - 0.5
        out_ref[:, lanes] = near_sum[0:3] - centre * near_sum[3:4]

    def gather(quad, part, picked):
        group = 4 * quad + part
        for k in range(NCELL):
            picked[part, k:k + 1, :] = table_ref[rows_smem[group, k]]

    def multipole(quad, part, picked):
        group = 4 * quad + part
        turned = picked[part].T
        lane_group = (cells_ref[pl.ds(group, 1), :] // 16) % 8
        feat = turned[0:16]
        for j in range(1, 8):
            feat = jnp.where(lane_group == j, turned[16 * j:16 * j + 16], feat)
        xyz = columns[2 * quad + part // 2, (part % 2) * 64:(part % 2) * 64 + 64, :]
        dx = xyz[:, 0:1] - feat[1:2]
        dy = xyz[:, 1:2] - feat[2:3]
        dz = xyz[:, 2:3] - feat[3:4]
        h = dx * dx + dy * dy + dz * dz + EPS
        inv = lax.rsqrt(h)
        inv2 = inv * inv
        inv3 = inv * inv2
        inv5 = inv3 * inv2
        qx = feat[4:5] * dx + feat[7:8] * dy + feat[8:9] * dz
        qy = feat[7:8] * dx + feat[5:6] * dy + feat[9:10] * dz
        qz = feat[8:9] * dx + feat[9:10] * dy + feat[6:7] * dz
        form = dx * qx + dy * qy + dz * qz
        along = feat[0:1] * inv3 + (2.5 * form) * (inv5 * inv2)
        pieces = []
        for d, q in ((dx, qx), (dy, qy), (dz, qz)):
            pieces.extend(split2(inv5 * q - along * d))
        return jnp.concatenate(pieces, axis=1)

    def cells_pull(quad, picked, later, later_picked):
        pieces = []
        for part in range(4):
            gather(later, part, later_picked)
            pieces.append(multipole(quad, part, picked))
        far_sum = nt(summing, jnp.concatenate(pieces, axis=0))
        lanes = quad_lanes(quad)
        out_ref[:, lanes] = out_ref[:, lanes] + far_sum[0:3]

    quads = PAIRS // 2
    first_weights = target_weights(0)
    for part in range(4):
        distances(0, part, first_weights, dist_a)

    def direct_two(i, _):
        for when, stage in STAGE_AT:
            @pl.when(i == when)
            def _():
                finish_stage(stage)
                start_stage(stage + 1)
        direct(2 * i, dist_a, 2 * i + 1, dist_b)
        direct(2 * i + 1, dist_b, jnp.minimum(2 * i + 2, quads - 1), dist_a)
        return 0

    lax.fori_loop(0, quads // 2, direct_two, 0)
    row_copy.wait()
    finish_stage(3)
    for part in range(4):
        gather(0, part, picked_a)

    def cells_two(i, _):
        cells_pull(2 * i, picked_a, 2 * i + 1, picked_b)
        cells_pull(2 * i + 1, picked_b, jnp.minimum(2 * i + 2, quads - 1), picked_a)
        return 0

    lax.fori_loop(0, quads // 2, cells_two, 0)

    for copy in near + far:
        copy.wait_send()
    for stage in range(3):
        for part in range(n_parts):
            for copy in stage_copies(part, stage):
                copy.wait_send()
    for part in range(n_parts):
        core_copy(part).wait_send()


def on_device(
    positions, masses, cell_mass, cell_center, cell_quad, cell_list, leaf_list, send_list, send_count,
):
    dma = pltpu.SemaphoreType.DMA
    n_off = len(OFFSETS)
    n_parts = len(PARTS)
    return pl.pallas_call(
        kernel,
        name="tree_pull",
        out_shape=jax.ShapeDtypeStruct((3, PAIRS * 128), F32),
        in_specs=[pl.BlockSpec(memory_space=pl.ANY)] * 9,
        out_specs=pl.BlockSpec(memory_space=pltpu.VMEM),
        scratch_shapes=[
            pltpu.VMEM((3, PAIRS * 128), F32),
            pltpu.VMEM((PAIRS, 128), F32),
            pltpu.VMEM((1, 128), F32),
            pltpu.VMEM((3, 128), F32),
            pltpu.VMEM((6, 128), F32),
            pltpu.VMEM((128, 128), jnp.int32),
            pltpu.SMEM((NLEAF, 128), jnp.int32),
            pltpu.SMEM((n_off, CAP), jnp.int32),
            pltpu.SMEM((n_off,), jnp.int32),
            pltpu.VMEM((128, 128), F32),
            pltpu.VMEM((PAIRS, 4, 128), F32),
            pltpu.VMEM((n_off, CAP // 2, 4, 128), F32),
            pltpu.VMEM((ALL_PAIRS, 4, 128), F32),
            pltpu.VMEM((N_CELL_ROWS, 1, 128), F32),
            pltpu.VMEM((2 * ALL_PAIRS, 64, 128), BF16),
            pltpu.VMEM((2 * ALL_PAIRS, 16, 128), BF16),
            pltpu.VMEM((PAIRS, 64, 128), BF16),
            pltpu.VMEM((PAIRS, 128, 8), F32),
            pltpu.VMEM((128, 128), jnp.int32),
            pltpu.SMEM((128, 128), jnp.int32),
            pltpu.VMEM((4, 128, 128), F32),
            pltpu.VMEM((4, 128, 128), F32),
            pltpu.VMEM((4, 256, 256), F32),
            pltpu.VMEM((4, 256, 256), F32),
            dma((9,)), dma,
            dma((NY,)), dma((NY,)), dma((n_off,)), dma((n_off,)),
            dma((n_parts, 3, NZ)), dma((n_parts, 3, NZ)), dma((n_parts,)), dma((n_parts,)),
        ],
        compiler_params=pltpu.CompilerParams(
            collective_id=0, has_side_effects=True, vmem_limit_bytes=60 * 1024 * 1024),
    )(
        positions, masses.reshape(PAIRS, 128), cell_mass.reshape(1, 128), cell_center, cell_quad,
        cell_list, leaf_list.T, send_list.reshape(2 * RANGE, CAP), send_count.reshape(2 * RANGE))


def solution(mesh):
    return jax.shard_map(
        on_device,
        mesh=mesh,
        in_specs=(
            P(None, ("dom", "sub")),
            P(("dom", "sub")),
            P(("dom", "sub")),
            P(None, ("dom", "sub")),
            P(None, ("dom", "sub")),
            P(("dom", "sub"), None),
            P(("dom", "sub"), None),
            P("dom", "sub", None, None),
            P("dom", "sub", None),
        ),
        out_specs=P(None, ("dom", "sub")),
        check_vma=False,
    )
```

```python
import functools

import jax
import jax.numpy as jnp
from jax import lax
from jax.experimental import pallas as pl
from jax.experimental.pallas import tpu as pltpu
from jax.sharding import PartitionSpec as P

LEAF = 64
NCELL = 128
NLEAF = 16
RANGE = 4
CAP = 8
EPS = 0.0025
F32 = jnp.float32
BF16 = jnp.bfloat16
MESH = pl.DeviceIdType.MESH

NX, NY, NZ, NCORE = 4, 4, 8, 2
SIZES = {"x": NX, "y": NY, "z": NZ}
ROWS = 16
PARTS = ((0, 8, ("z", "x", "y")), (8, 8, ("z", "y", "x")))
OFFSETS = tuple(range(-RANGE, 0)) + tuple(range(1, RANGE + 1))
PAIRS = 64
ALL_PAIRS = NY * PAIRS + len(OFFSETS) * CAP // 2
N_CELL_ROWS = NX * NY * NZ * NCORE * ROWS
N_SLOTS = 8
CHUNK = 16
STAGE_AT = ((0, 1), (8, 2))


def split3(value):
    high = value.astype(BF16).astype(F32)
    rest = value - high
    mid = rest.astype(BF16).astype(F32)
    return high, mid, rest - mid


def split2(value):
    high = value.astype(BF16)
    return high, (value - high.astype(F32)).astype(BF16)


def nt(a, b):
    return lax.dot_general(a, b, (((1,), (1,)), ((), ())), preferred_element_type=F32)


def cell_row(cell):
    shard = cell // 128
    sub = shard % NY
    dom = shard // NY
    at = {"x": dom // (NZ * NCORE), "z": (dom // NCORE) % NZ, "y": sub}
    core = dom % NCORE
    row = cell % 16
    n = N_CELL_ROWS // ROWS
    result = None
    for first, rows, order in PARTS:
        index, stride = 0, 1
        for axis in order:
            index = index + at[axis] * stride
            stride = stride * SIZES[axis]
        index = index + core * stride
        here = n * first + index * rows + (row - first)
        result = here if result is None else jnp.where(row >= first, here, result)
    return result


def kernel(
    pos_hbm, mass_hbm, cmass_hbm, ccen_hbm, cquad_hbm, cells_hbm, leaf_hbm, list_hbm, count_hbm,
    out_ref,
    pos_ref, mass_ref, cmass_ref, ccen_ref, cquad_ref, cells_ref, leaf_ids, send_list, send_count,
    pad, own, far_out, leaf_ref, table_ref,
    features, moments, targets, columns, rows_vmem, rows_smem, picked_a, picked_b, feat_a, feat_b, pieces_a, pieces_b,
    dist_a, dist_b,
    load_sem, row_sem, near_send, near_recv, far_send, far_recv, cell_send, cell_recv, core_send, core_recv,
):
    dom = lax.axis_index("dom")
    sub = lax.axis_index("sub")
    core = dom % NCORE
    at = {"x": dom // (NZ * NCORE), "z": (dom // NCORE) % NZ, "y": sub}
    n_dom = NX * NZ * NCORE
    base = sub * PAIRS

    loads = [
        pltpu.make_async_copy(src, dst, load_sem.at[i])
        for i, (src, dst) in enumerate((
            (pos_hbm, pos_ref), (mass_hbm, mass_ref), (cmass_hbm, cmass_ref), (ccen_hbm, ccen_ref),
            (cquad_hbm, cquad_ref), (list_hbm, send_list), (count_hbm, send_count), (cells_hbm, cells_ref),
            (leaf_hbm, leaf_ids)))
    ]
    for load in loads:
        load.start()

    def device(x, y, z, c):
        return ((x * NZ + z) * NCORE + c, y)

    def peer(axis, step):
        where = dict(at)
        where[axis] = (at[axis] + step) % SIZES[axis]
        return device(where["x"], where["y"], where["z"], core)

    barrier = pltpu.get_barrier_semaphore()
    waits = 0
    for axis in ("x", "y", "z"):
        for step in range(1, SIZES[axis]):
            pl.semaphore_signal(barrier, inc=1, device_id=peer(axis, step), device_id_type=MESH)
            waits += 1
    other_core = device(at["x"], at["y"], at["z"], 1 - core)
    pl.semaphore_signal(barrier, inc=1, device_id=other_core, device_id_type=MESH)
    waits += 1
    for off in OFFSETS:
        pl.semaphore_signal(barrier, inc=1, device_id=((dom + off + n_dom) % n_dom, sub), device_id_type=MESH)
        waits += 1

    for load in loads[0:5]:
        load.wait()
    for j in range(PAIRS):
        own[j, 0:3, :] = pos_ref[:, j * 128:(j + 1) * 128]
        own[j, 3:4, :] = mass_ref[j:j + 1, :]
    pad[...] = jnp.zeros((128, 128), F32)
    pad[0:1, :] = cmass_ref[...]
    pad[1:4, :] = ccen_ref[...]
    pad[4:10, :] = cquad_ref[...]
    by_cell = pad[...].T
    packed = by_cell[0:16, :]
    for g in range(1, 8):
        packed = packed + pltpu.roll(by_cell[16 * g:16 * g + 16, :], 16 * g, 1)
    pad[0:16, :] = packed

    def start_of(part, done):
        first, rows, order = PARTS[part]
        size = rows
        n = N_CELL_ROWS // ROWS
        index = 0
        stride = 1
        for s, axis in enumerate(order):
            if s >= done:
                index = index + at[axis] * stride
            stride = stride * SIZES[axis]
        index = index + core * stride
        for axis in order[:done]:
            size = size * SIZES[axis]
        return n * first + index * rows, size

    for part, (first, rows, order) in enumerate(PARTS):
        start, _ = start_of(part, 0)
        for r in range(rows):
            table_ref[start + r, :, :] = pad[first + r:first + r + 1, :]

    row8 = lax.broadcasted_iota(jnp.int32, (8, 128), 0)
    one_row = jnp.where(row8 == 4, 1.0, 0.0).astype(F32)
    no_rows = jnp.zeros((16, 128), F32)

    def prepare(source_ref, source, pair):
        raw4 = source_ref[source]
        raw = jnp.concatenate([raw4, raw4], axis=0)
        mass = raw4[3:4, :]
        centred = raw - 0.5
        square = jnp.where(row8 < 3, centred * centred, 0.0)
        norm = jnp.sum(square, axis=0, keepdims=True) + EPS
        u = jnp.where(row8 < 3, centred, jnp.where(row8 == 3, norm, one_row))
        s = jnp.where(row8 < 3, centred * mass, jnp.where(row8 == 3, mass, 0.0))
        u_high, u_mid, u_low = split3(u)
        s_high, s_mid, s_low = split3(s)
        s_full = jnp.concatenate([s_high + pltpu.roll(s_mid, 4, 0), s_low], axis=0)
        moments[2 * pair] = s_full.astype(BF16)
        moments[2 * pair + 1] = pltpu.roll(s_full, LEAF, 1).astype(BF16)
        u_full = jnp.concatenate([u_high, u_mid, u_high, u_mid, u_high, u_low, no_rows], axis=0).astype(BF16)
        turned = jnp.concatenate([u_full, u_full], axis=0).T
        features[2 * pair] = turned[0:64]
        features[2 * pair + 1] = turned[64:128]

    def prepare_range(source_ref, source, pair, count):
        def body(j, _):
            prepare(source_ref, source + j, pair + j)
            return 0
        lax.fori_loop(0, count, body, 0, unroll=8)

    def prepare_targets(pair, _):
        raw3 = pos_ref[:, pl.ds(pl.multiple_of(pair * 128, 128), 128)]
        raw = jnp.concatenate([raw3, jnp.zeros((5, 128), F32)], axis=0)
        centred = raw - 0.5
        square = jnp.where(row8 < 3, centred * centred, 0.0)
        norm = jnp.sum(square, axis=0, keepdims=True)
        t = jnp.where(row8 < 3, -2.0 * centred,
                      jnp.where(row8 == 3, 1.0, jnp.where(row8 == 4, norm, 0.0)))
        t_high, t_mid, t_low = split3(t)
        targets[pair] = jnp.concatenate(
            [t_high, t_high, t_mid, t_mid, t_low, t_high, no_rows], axis=0).astype(BF16)
        columns[pair] = jnp.concatenate([raw, jnp.zeros((120, 128), F32)], axis=0).T[:, 0:8]
        return 0

    prepare_range(own, 0, base, PAIRS)
    lax.fori_loop(0, PAIRS, prepare_targets, 0, unroll=8)
    for load in loads[7:9]:
        load.wait()
    cells = cells_ref[...]
    found = cell_row(cells)
    for quad in range(PAIRS // 2):
        rows_vmem[quad] = found[4 * quad:4 * quad + 4]
    cells_ref[...] = (cells >> 4) & 7

    def row_copy(quad, slot):
        return pltpu.make_async_copy(rows_vmem.at[quad], rows_smem[slot], row_sem.at[slot])

    row_copy(0, N_SLOTS - 1).start()
    for slot in range(N_SLOTS - 1):
        row_copy(slot + 1, slot).start()

    pl.semaphore_wait(barrier, waits)

    def cell_copy(part, stage, step):
        axis = PARTS[part][2][stage]
        start, size = start_of(part, stage)
        block = table_ref.at[pl.ds(start, size)]
        return pltpu.make_async_remote_copy(
            src_ref=block, dst_ref=block,
            send_sem=cell_send.at[part, stage, step], recv_sem=cell_recv.at[part, stage, step],
            device_id=peer(axis, step), device_id_type=MESH)

    def stage_copies(part, stage):
        return [cell_copy(part, stage, step) for step in range(1, SIZES[PARTS[part][2][stage]])]

    def core_copy(part):
        start, size = start_of(part, 3)
        block = table_ref.at[pl.ds(start, size)]
        return pltpu.make_async_remote_copy(
            src_ref=block, dst_ref=block, send_sem=core_send.at[part], recv_sem=core_recv.at[part],
            device_id=other_core, device_id_type=MESH)

    n_parts = len(PARTS)

    def start_stage(stage):
        for part in range(n_parts):
            if stage == 3:
                core_copy(part).start()
            else:
                for copy in stage_copies(part, stage):
                    copy.start()

    def finish_stage(stage):
        for part in range(n_parts):
            if stage == 3:
                core_copy(part).wait_recv()
            else:
                for copy in stage_copies(part, stage):
                    copy.wait_recv()

    near = [
        pltpu.make_async_remote_copy(
            src_ref=own, dst_ref=leaf_ref.at[pl.ds(base, PAIRS)],
            send_sem=near_send.at[step], recv_sem=near_recv.at[step],
            device_id=peer("y", step), device_id_type=MESH)
        for step in range(1, NY)
    ]
    for copy in near:
        copy.start()
    start_stage(0)

    for load in loads[5:7]:
        load.wait()
    low_half4 = lax.broadcasted_iota(jnp.int32, (4, 128), 1) < LEAF

    def far_pair(slot, t):
        halves = []
        for h in range(2):
            block = send_list[slot, 2 * t + h]
            tile = own[block // 2]
            turned = pltpu.roll(tile, LEAF, 1)
            picked = jnp.where(block % 2 == h, tile, turned)
            inside = jnp.logical_and(dom + OFFSETS[slot] >= 0, dom + OFFSETS[slot] < n_dom)
            live = jnp.logical_and(inside, 2 * t + h < send_count[slot])
            halves.append(jnp.where(live, picked, jnp.zeros_like(picked)))
        far_out[slot, t] = jnp.where(low_half4, halves[0], halves[1])

    def far_copy(slot):
        return pltpu.make_async_remote_copy(
            src_ref=far_out.at[slot],
            dst_ref=leaf_ref.at[pl.ds(NY * PAIRS + slot * (CAP // 2), CAP // 2)],
            send_sem=far_send.at[slot], recv_sem=far_recv.at[slot],
            device_id=((dom + OFFSETS[slot] + n_dom) % n_dom, sub), device_id_type=MESH)

    for slot in range(len(OFFSETS)):
        for t in range(CAP // 2):
            far_pair(slot, t)
    far = [far_copy(slot) for slot in range(len(OFFSETS))]
    for copy in far:
        copy.start()

    finish_stage(0)
    start_stage(1)
    for copy in far:
        copy.wait_recv()
    prepare_range(leaf_ref, NY * PAIRS, NY * PAIRS, len(OFFSETS) * CAP // 2)
    for step in range(1, NY):
        near[step - 1].wait_recv()
        origin = ((sub + NY - step) % NY) * PAIRS
        prepare_range(leaf_ref, origin, origin, PAIRS)

    low_half = lax.broadcasted_iota(jnp.int32, (64, 128), 1) < LEAF
    low_half16 = lax.broadcasted_iota(jnp.int32, (16, 128), 1) < LEAF
    summing_row = lax.broadcasted_iota(jnp.int32, (8, 768), 0)
    summing_lane = lax.broadcasted_iota(jnp.int32, (8, 768), 1)
    summing = jnp.where(summing_row == (summing_lane // 256), 1.0, 0.0).astype(BF16)
    lane_block = lax.broadcasted_iota(jnp.int32, (8, 256), 1) // LEAF
    nothing = jnp.zeros((64, 128), BF16)
    empty = jnp.zeros((128, 128), BF16)

    def target_weights(quad):
        blocks = []
        for half in range(2):
            tile = targets[2 * quad + half]
            diagonal = jnp.concatenate(
                [jnp.where(low_half, tile, nothing), jnp.where(low_half, nothing, tile)], axis=0)
            blocks.append(jnp.concatenate([diagonal, empty] if half == 0 else [empty, diagonal], axis=0))
        return jnp.concatenate(blocks, axis=1)

    def distances(quad, part, weights, dist):
        rows = []
        for slot in range(4 * part, 4 * part + 4):
            halves = []
            for half in range(2):
                first = leaf_ids[slot, 4 * quad + 2 * half]
                second = leaf_ids[slot, 4 * quad + 2 * half + 1]
                halves.append(jnp.where(low_half, features[first], features[second]))
            rows.append(jnp.concatenate(halves, axis=1))
        lhs = jnp.concatenate(rows, axis=0)
        dist[part] = jnp.dot(lhs, weights, preferred_element_type=F32)

    def weigh(quad, part, dist, totals):
        inv = lax.rsqrt(dist[part])
        w_high, w_low = split2(inv * inv * inv)
        rows = []
        for j in range(4):
            group = 4 * quad + j
            tiles = []
            for slot in range(4 * part, 4 * part + 4, 2):
                low = leaf_ids[slot, group]
                high = leaf_ids[slot + 1, group]
                tiles.append(jnp.where(low_half16, moments[low], moments[high ^ 1]))
            rows.append(jnp.concatenate(tiles, axis=1))
        full = jnp.concatenate(rows, axis=0)
        short = jnp.concatenate([row[0:8] for row in rows], axis=0)
        high = jnp.dot(full, w_high, preferred_element_type=F32)
        low = jnp.dot(short, w_low, preferred_element_type=F32)
        if totals is None:
            return high, low
        return totals[0] + high, totals[1] + low

    def quad_lanes(quad):
        return pl.ds(pl.multiple_of(quad * 256, 256), 256)

    def direct(quad, dist, later, later_dist):
        totals = None
        weights = target_weights(later)
        for part in range(4):
            distances(later, part, weights, later_dist)
            totals = weigh(quad, part, dist, totals)
        high, low = totals
        near_sum = jnp.zeros((8, 256), F32)
        for j in range(4):
            block = high[16 * j:16 * j + 8] + high[16 * j + 8:16 * j + 16] + low[8 * j:8 * j + 8]
            near_sum = jnp.where(lane_block == j, block, near_sum)
        near_sum = near_sum + pltpu.roll(near_sum, 4, 0)
        lanes = quad_lanes(quad)
        centre = pos_ref[:, lanes] - 0.5
        out_ref[:, lanes] = near_sum[0:3] - centre * near_sum[3:4]

    def gather(slot, part, start, count, picked):
        rows = rows_smem[slot]
        for k in range(start, start + count):
            row = table_ref[rows[part, k]]
            picked[part, k:k + 1, :] = row
        return row

    def cell_features(quad, part, picked, feat_ref):
        turned = picked[part].T
        lane_group = cells_ref[pl.ds(4 * quad + part, 1), :]
        feat = turned[0:16]
        for j in range(1, 8):
            feat = jnp.where(lane_group == j, turned[16 * j:16 * j + 16], feat)
        feat_ref[part] = feat

    def multipole(quad, part, start, feat_ref, pieces, after):
        first = (part % 2) * 64 + start
        xyz = columns[2 * quad + part // 2, first:first + CHUNK, :]
        feat = [feat_ref[part, f:f + 1, :] for f in range(10)]
        if after is not None:
            feat[9] = feat[9] + after * 0.0
        dx = xyz[:, 0:1] - feat[1]
        dy = xyz[:, 1:2] - feat[2]
        dz = xyz[:, 2:3] - feat[3]
        h = dx * dx + dy * dy + dz * dz + EPS
        inv = lax.rsqrt(h)
        inv2 = inv * inv
        inv5 = inv2 * inv2 * inv
        qx = feat[4] * dx + feat[7] * dy + feat[8] * dz
        qy = feat[7] * dx + feat[5] * dy + feat[9] * dz
        qz = feat[8] * dx + feat[9] * dy + feat[6] * dz
        form = dx * qx + dy * qy + dz * qz
        along = feat[0] * h + (2.5 * form) * inv2
        row = part * 64 + start
        for c, (d, q) in enumerate(((dx, qx), (dy, qy), (dz, qz))):
            high, low = split2(inv5 * (q - along * d))
            pieces[row:row + CHUNK, 256 * c:256 * c + 128] = high
            pieces[row:row + CHUNK, 256 * c + 128:256 * c + 256] = low

    def cells_pull(quad, feat_ref, pieces, later, slot, later_picked, later_feat, after):
        steps = LEAF // CHUNK
        for part in range(4):
            for c in range(steps):
                fetched = gather(slot, part, c * (NCELL // steps), NCELL // steps, later_picked)
                multipole(quad, part, c * CHUNK, feat_ref, pieces, after)
                after = fetched
            cell_features(later, part, later_picked, later_feat)
        far_sum = nt(summing, pieces[...])
        lanes = quad_lanes(quad)
        out_ref[:, lanes] = out_ref[:, lanes] + far_sum[0:3]
        return after

    quads = PAIRS // 2
    first_weights = target_weights(0)
    for part in range(4):
        distances(0, part, first_weights, dist_a)

    def direct_two(i, _):
        for when, stage in STAGE_AT:
            @pl.when(i == when)
            def _():
                finish_stage(stage)
                start_stage(stage + 1)
        direct(2 * i, dist_a, 2 * i + 1, dist_b)
        direct(2 * i + 1, dist_b, jnp.minimum(2 * i + 2, quads - 1), dist_a)
        return 0

    lax.fori_loop(0, quads // 2, direct_two, 0)
    finish_stage(3)
    row_copy(0, N_SLOTS - 1).wait()
    for part in range(4):
        gather(N_SLOTS - 1, part, 0, NCELL, picked_a)
        cell_features(0, part, picked_a, feat_a)
    row_copy(N_SLOTS, N_SLOTS - 1).start()

    def cells_some(i, _):
        for block in range(0, N_SLOTS, 4):
            for slot in range(block, block + 4):
                row_copy(0, slot).wait()
            after = None
            for slot in range(block, block + 4):
                quad = N_SLOTS * i + slot
                later = jnp.minimum(quad + 1, quads - 1)
                if slot % 2 == 0:
                    after = cells_pull(quad, feat_a, pieces_a, later, slot, picked_b, feat_b, after)
                else:
                    after = cells_pull(quad, feat_b, pieces_b, later, slot, picked_a, feat_a, after)
            for slot in range(block, block + 4):
                row_copy(jnp.minimum(N_SLOTS * (i + 1) + slot + 1, quads - 1), slot).start()
        return 0

    lax.fori_loop(0, quads // N_SLOTS, cells_some, 0)
    for slot in range(N_SLOTS):
        row_copy(0, slot).wait()

    for copy in near + far:
        copy.wait_send()
    for stage in range(3):
        for part in range(n_parts):
            for copy in stage_copies(part, stage):
                copy.wait_send()
    for part in range(n_parts):
        core_copy(part).wait_send()


def on_device(
    positions, masses, cell_mass, cell_center, cell_quad, cell_list, leaf_list, send_list, send_count,
):
    dma = pltpu.SemaphoreType.DMA
    n_off = len(OFFSETS)
    n_parts = len(PARTS)
    return pl.pallas_call(
        kernel,
        name="tree_pull",
        out_shape=jax.ShapeDtypeStruct((3, PAIRS * 128), F32),
        in_specs=[pl.BlockSpec(memory_space=pl.ANY)] * 9,
        out_specs=pl.BlockSpec(memory_space=pltpu.VMEM),
        scratch_shapes=[
            pltpu.VMEM((3, PAIRS * 128), F32),
            pltpu.VMEM((PAIRS, 128), F32),
            pltpu.VMEM((1, 128), F32),
            pltpu.VMEM((3, 128), F32),
            pltpu.VMEM((6, 128), F32),
            pltpu.VMEM((128, 128), jnp.int32),
            pltpu.SMEM((NLEAF, 128), jnp.int32),
            pltpu.SMEM((n_off, CAP), jnp.int32),
            pltpu.SMEM((n_off,), jnp.int32),
            pltpu.VMEM((128, 128), F32),
            pltpu.VMEM((PAIRS, 4, 128), F32),
            pltpu.VMEM((n_off, CAP // 2, 4, 128), F32),
            pltpu.VMEM((ALL_PAIRS, 4, 128), F32),
            pltpu.VMEM((N_CELL_ROWS, 1, 128), F32),
            pltpu.VMEM((2 * ALL_PAIRS, 64, 128), BF16),
            pltpu.VMEM((2 * ALL_PAIRS, 16, 128), BF16),
            pltpu.VMEM((PAIRS, 64, 128), BF16),
            pltpu.VMEM((PAIRS, 128, 8), F32),
            pltpu.VMEM((PAIRS // 2, 4, 128), jnp.int32),
            [pltpu.SMEM((4, 128), jnp.int32) for _ in range(N_SLOTS)],
            pltpu.VMEM((4, 128, 128), F32),
            pltpu.VMEM((4, 128, 128), F32),
            pltpu.VMEM((4, 16, 128), F32),
            pltpu.VMEM((4, 16, 128), F32),
            pltpu.VMEM((256, 768), BF16),
            pltpu.VMEM((256, 768), BF16),
            pltpu.VMEM((4, 256, 256), F32),
            pltpu.VMEM((4, 256, 256), F32),
            dma((9,)), dma((N_SLOTS,)),
            dma((NY,)), dma((NY,)), dma((n_off,)), dma((n_off,)),
            dma((n_parts, 3, NZ)), dma((n_parts, 3, NZ)), dma((n_parts,)), dma((n_parts,)),
        ],
        compiler_params=pltpu.CompilerParams(
            collective_id=0, has_side_effects=True, vmem_limit_bytes=60 * 1024 * 1024),
    )(
        positions, masses.reshape(PAIRS, 128), cell_mass.reshape(1, 128), cell_center, cell_quad,
        cell_list, leaf_list.T, send_list.reshape(2 * RANGE, CAP), send_count.reshape(2 * RANGE))


def solution(mesh):
    return jax.shard_map(
        on_device,
        mesh=mesh,
        in_specs=(
            P(None, ("dom", "sub")),
            P(("dom", "sub")),
            P(("dom", "sub")),
            P(None, ("dom", "sub")),
            P(None, ("dom", "sub")),
            P(("dom", "sub"), None),
            P(("dom", "sub"), None),
            P("dom", "sub", None, None),
            P("dom", "sub", None),
        ),
        out_specs=P(None, ("dom", "sub")),
        check_vma=False,
    )
```

```python
import functools

import jax
import jax.numpy as jnp
from jax import lax
from jax.experimental import pallas as pl
from jax.experimental.pallas import tpu as pltpu
from jax.sharding import PartitionSpec as P

LEAF = 64
NCELL = 128
NLEAF = 16
RANGE = 4
CAP = 8
EPS = 0.0025
F32 = jnp.float32
BF16 = jnp.bfloat16
MESH = pl.DeviceIdType.MESH

NX, NY, NZ, NCORE = 4, 4, 8, 2
SIZES = {"x": NX, "y": NY, "z": NZ}
ROWS = 16
PARTS = ((0, 8, ("z", "x", "y")), (8, 8, ("z", "y", "x")))
OFFSETS = tuple(range(-RANGE, 0)) + tuple(range(1, RANGE + 1))
PAIRS = 64
ALL_PAIRS = NY * PAIRS + len(OFFSETS) * CAP // 2
N_CELL_ROWS = NX * NY * NZ * NCORE * ROWS
N_SLOTS = 8
LAG = 2
CHUNK = 32
STAGE_AT = ((0, 1), (4, 2))


def split3(value):
    high = value.astype(BF16).astype(F32)
    rest = value - high
    mid = rest.astype(BF16).astype(F32)
    return high, mid, rest - mid


def split2(value):
    high = value.astype(BF16)
    return high, (value - high.astype(F32)).astype(BF16)


def nt(a, b):
    return lax.dot_general(a, b, (((1,), (1,)), ((), ())), preferred_element_type=F32)


def cell_row(cell):
    shard = cell // 128
    sub = shard % NY
    dom = shard // NY
    at = {"x": dom // (NZ * NCORE), "z": (dom // NCORE) % NZ, "y": sub}
    core = dom % NCORE
    row = cell % 16
    n = N_CELL_ROWS // ROWS
    result = None
    for first, rows, order in PARTS:
        index, stride = 0, 1
        for axis in order:
            index = index + at[axis] * stride
            stride = stride * SIZES[axis]
        index = index + core * stride
        here = n * first + index * rows + (row - first)
        result = here if result is None else jnp.where(row >= first, here, result)
    return result


def kernel(
    pos_hbm, mass_hbm, cmass_hbm, ccen_hbm, cquad_hbm, cells_hbm, leaf_hbm, list_hbm, count_hbm,
    out_ref,
    pos_ref, mass_ref, cmass_ref, ccen_ref, cquad_ref, cells_ref, leaf_ids, send_list, send_count,
    pad, own, far_out, leaf_ref, table_ref,
    features, moments, targets, columns, rows_vmem, rows_smem, picked_a, picked_b, feat_a, feat_b, pieces_a, pieces_b,
    dist_a, dist_b,
    load_sem, row_sem, near_send, near_recv, far_send, far_recv, cell_send, cell_recv, core_send, core_recv,
):
    dom = lax.axis_index("dom")
    sub = lax.axis_index("sub")
    core = dom % NCORE
    at = {"x": dom // (NZ * NCORE), "z": (dom // NCORE) % NZ, "y": sub}
    n_dom = NX * NZ * NCORE
    base = sub * PAIRS

    loads = [
        pltpu.make_async_copy(src, dst, load_sem.at[i])
        for i, (src, dst) in enumerate((
            (pos_hbm, pos_ref), (mass_hbm, mass_ref), (cmass_hbm, cmass_ref), (ccen_hbm, ccen_ref),
            (cquad_hbm, cquad_ref), (list_hbm, send_list), (count_hbm, send_count), (cells_hbm, cells_ref),
            (leaf_hbm, leaf_ids)))
    ]
    for load in loads:
        load.start()

    def device(x, y, z, c):
        return ((x * NZ + z) * NCORE + c, y)

    def peer(axis, step):
        where = dict(at)
        where[axis] = (at[axis] + step) % SIZES[axis]
        return device(where["x"], where["y"], where["z"], core)

    barrier = pltpu.get_barrier_semaphore()
    waits = 0
    for axis in ("x", "y", "z"):
        for step in range(1, SIZES[axis]):
            pl.semaphore_signal(barrier, inc=1, device_id=peer(axis, step), device_id_type=MESH)
            waits += 1
    other_core = device(at["x"], at["y"], at["z"], 1 - core)
    pl.semaphore_signal(barrier, inc=1, device_id=other_core, device_id_type=MESH)
    waits += 1
    for off in OFFSETS:
        pl.semaphore_signal(barrier, inc=1, device_id=((dom + off + n_dom) % n_dom, sub), device_id_type=MESH)
        waits += 1

    for load in loads[0:5]:
        load.wait()
    for j in range(PAIRS):
        own[j, 0:3, :] = pos_ref[:, j * 128:(j + 1) * 128]
        own[j, 3:4, :] = mass_ref[j:j + 1, :]
    pad[...] = jnp.zeros((128, 128), F32)
    pad[0:1, :] = cmass_ref[...]
    pad[1:4, :] = ccen_ref[...]
    pad[4:10, :] = cquad_ref[...]
    by_cell = pad[...].T
    packed = by_cell[0:16, :]
    for g in range(1, 8):
        packed = packed + pltpu.roll(by_cell[16 * g:16 * g + 16, :], 16 * g, 1)
    pad[0:16, :] = packed

    def start_of(part, done):
        first, rows, order = PARTS[part]
        size = rows
        n = N_CELL_ROWS // ROWS
        index = 0
        stride = 1
        for s, axis in enumerate(order):
            if s >= done:
                index = index + at[axis] * stride
            stride = stride * SIZES[axis]
        index = index + core * stride
        for axis in order[:done]:
            size = size * SIZES[axis]
        return n * first + index * rows, size

    for part, (first, rows, order) in enumerate(PARTS):
        start, _ = start_of(part, 0)
        for r in range(rows):
            table_ref[start + r, :, :] = pad[first + r:first + r + 1, :]

    row8 = lax.broadcasted_iota(jnp.int32, (8, 128), 0)
    one_row = jnp.where(row8 == 4, 1.0, 0.0).astype(F32)
    no_rows = jnp.zeros((16, 128), F32)

    def prepare(source_ref, source, pair):
        raw4 = source_ref[source]
        raw = jnp.concatenate([raw4, raw4], axis=0)
        mass = raw4[3:4, :]
        centred = raw - 0.5
        square = jnp.where(row8 < 3, centred * centred, 0.0)
        norm = jnp.sum(square, axis=0, keepdims=True) + EPS
        u = jnp.where(row8 < 3, centred, jnp.where(row8 == 3, norm, one_row))
        s = jnp.where(row8 < 3, centred * mass, jnp.where(row8 == 3, mass, 0.0))
        u_high, u_mid, u_low = split3(u)
        s_high, s_mid, s_low = split3(s)
        s_full = jnp.concatenate([s_high + pltpu.roll(s_mid, 4, 0), s_low], axis=0)
        moments[2 * pair] = s_full.astype(BF16)
        moments[2 * pair + 1] = pltpu.roll(s_full, LEAF, 1).astype(BF16)
        u_full = jnp.concatenate([u_high, u_mid, u_high, u_mid, u_high, u_low, no_rows], axis=0).astype(BF16)
        turned = jnp.concatenate([u_full, u_full], axis=0).T
        features[2 * pair] = turned[0:64]
        features[2 * pair + 1] = turned[64:128]

    def prepare_range(source_ref, source, pair, count):
        def body(j, _):
            prepare(source_ref, source + j, pair + j)
            return 0
        lax.fori_loop(0, count, body, 0, unroll=8)

    def prepare_targets(pair, _):
        raw3 = pos_ref[:, pl.ds(pl.multiple_of(pair * 128, 128), 128)]
        raw = jnp.concatenate([raw3, jnp.zeros((5, 128), F32)], axis=0)
        centred = raw - 0.5
        square = jnp.where(row8 < 3, centred * centred, 0.0)
        norm = jnp.sum(square, axis=0, keepdims=True)
        t = jnp.where(row8 < 3, -2.0 * centred,
                      jnp.where(row8 == 3, 1.0, jnp.where(row8 == 4, norm, 0.0)))
        t_high, t_mid, t_low = split3(t)
        targets[pair] = jnp.concatenate(
            [t_high, t_high, t_mid, t_mid, t_low, t_high, no_rows], axis=0).astype(BF16)
        columns[pair] = jnp.concatenate([raw, jnp.zeros((120, 128), F32)], axis=0).T[:, 0:8]
        return 0

    prepare_range(own, 0, base, PAIRS)
    lax.fori_loop(0, PAIRS, prepare_targets, 0, unroll=8)
    for load in loads[7:9]:
        load.wait()
    cells = cells_ref[...]
    found = cell_row(cells)
    for quad in range(PAIRS // 2):
        rows_vmem[quad] = found[4 * quad:4 * quad + 4]
    cells_ref[...] = (cells >> 4) & 7

    def row_copy(quad, slot):
        return pltpu.make_async_copy(rows_vmem.at[quad], rows_smem[slot], row_sem.at[slot])

    row_copy(0, N_SLOTS - 1).start()
    for slot in range(N_SLOTS - 1):
        row_copy(slot + 1, slot).start()

    pl.semaphore_wait(barrier, waits)

    def cell_copy(part, stage, step):
        axis = PARTS[part][2][stage]
        start, size = start_of(part, stage)
        block = table_ref.at[pl.ds(start, size)]
        return pltpu.make_async_remote_copy(
            src_ref=block, dst_ref=block,
            send_sem=cell_send.at[part, stage, step], recv_sem=cell_recv.at[part, stage, step],
            device_id=peer(axis, step), device_id_type=MESH)

    def stage_copies(part, stage):
        return [cell_copy(part, stage, step) for step in range(1, SIZES[PARTS[part][2][stage]])]

    def core_copy(part):
        start, size = start_of(part, 3)
        block = table_ref.at[pl.ds(start, size)]
        return pltpu.make_async_remote_copy(
            src_ref=block, dst_ref=block, send_sem=core_send.at[part], recv_sem=core_recv.at[part],
            device_id=other_core, device_id_type=MESH)

    n_parts = len(PARTS)

    def start_stage(stage):
        for part in range(n_parts):
            if stage == 3:
                core_copy(part).start()
            else:
                for copy in stage_copies(part, stage):
                    copy.start()

    def finish_stage(stage):
        for part in range(n_parts):
            if stage == 3:
                core_copy(part).wait_recv()
            else:
                for copy in stage_copies(part, stage):
                    copy.wait_recv()

    near = [
        pltpu.make_async_remote_copy(
            src_ref=own, dst_ref=leaf_ref.at[pl.ds(base, PAIRS)],
            send_sem=near_send.at[step], recv_sem=near_recv.at[step],
            device_id=peer("y", step), device_id_type=MESH)
        for step in range(1, NY)
    ]
    for copy in near:
        copy.start()
    start_stage(0)

    for load in loads[5:7]:
        load.wait()
    low_half4 = lax.broadcasted_iota(jnp.int32, (4, 128), 1) < LEAF

    def far_pair(slot, t):
        halves = []
        for h in range(2):
            block = send_list[slot, 2 * t + h]
            tile = own[block // 2]
            turned = pltpu.roll(tile, LEAF, 1)
            picked = jnp.where(block % 2 == h, tile, turned)
            inside = jnp.logical_and(dom + OFFSETS[slot] >= 0, dom + OFFSETS[slot] < n_dom)
            live = jnp.logical_and(inside, 2 * t + h < send_count[slot])
            halves.append(jnp.where(live, picked, jnp.zeros_like(picked)))
        far_out[slot, t] = jnp.where(low_half4, halves[0], halves[1])

    def far_copy(slot):
        return pltpu.make_async_remote_copy(
            src_ref=far_out.at[slot],
            dst_ref=leaf_ref.at[pl.ds(NY * PAIRS + slot * (CAP // 2), CAP // 2)],
            send_sem=far_send.at[slot], recv_sem=far_recv.at[slot],
            device_id=((dom + OFFSETS[slot] + n_dom) % n_dom, sub), device_id_type=MESH)

    for slot in range(len(OFFSETS)):
        for t in range(CAP // 2):
            far_pair(slot, t)
    far = [far_copy(slot) for slot in range(len(OFFSETS))]
    for copy in far:
        copy.start()

    finish_stage(0)
    start_stage(1)
    for copy in far:
        copy.wait_recv()
    prepare_range(leaf_ref, NY * PAIRS, NY * PAIRS, len(OFFSETS) * CAP // 2)
    for step in range(1, NY):
        near[step - 1].wait_recv()
        origin = ((sub + NY - step) % NY) * PAIRS
        prepare_range(leaf_ref, origin, origin, PAIRS)

    low_half = lax.broadcasted_iota(jnp.int32, (64, 128), 1) < LEAF
    low_half16 = lax.broadcasted_iota(jnp.int32, (16, 128), 1) < LEAF
    summing_row = lax.broadcasted_iota(jnp.int32, (8, 768), 0)
    summing_lane = lax.broadcasted_iota(jnp.int32, (8, 768), 1)
    summing = jnp.where(summing_row == (summing_lane // 256), 1.0, 0.0).astype(BF16)
    lane_block = lax.broadcasted_iota(jnp.int32, (8, 256), 1) // LEAF
    nothing = jnp.zeros((64, 128), BF16)
    empty = jnp.zeros((128, 128), BF16)

    def target_weights(quad):
        blocks = []
        for half in range(2):
            tile = targets[2 * quad + half]
            diagonal = jnp.concatenate(
                [jnp.where(low_half, tile, nothing), jnp.where(low_half, nothing, tile)], axis=0)
            blocks.append(jnp.concatenate([diagonal, empty] if half == 0 else [empty, diagonal], axis=0))
        return jnp.concatenate(blocks, axis=1)

    def distances(quad, part, weights, dist):
        rows = []
        for slot in range(4 * part, 4 * part + 4):
            halves = []
            for half in range(2):
                first = leaf_ids[slot, 4 * quad + 2 * half]
                second = leaf_ids[slot, 4 * quad + 2 * half + 1]
                halves.append(jnp.where(low_half, features[first], features[second]))
            rows.append(jnp.concatenate(halves, axis=1))
        lhs = jnp.concatenate(rows, axis=0)
        dist[part] = jnp.dot(lhs, weights, preferred_element_type=F32)

    def weigh(quad, part, dist, totals):
        inv = lax.rsqrt(dist[part])
        w_high, w_low = split2(inv * inv * inv)
        rows = []
        for j in range(4):
            group = 4 * quad + j
            tiles = []
            for slot in range(4 * part, 4 * part + 4, 2):
                low = leaf_ids[slot, group]
                high = leaf_ids[slot + 1, group]
                tiles.append(jnp.where(low_half16, moments[low], moments[high ^ 1]))
            rows.append(jnp.concatenate(tiles, axis=1))
        full = jnp.concatenate(rows, axis=0)
        short = jnp.concatenate([row[0:8] for row in rows], axis=0)
        high = jnp.dot(full, w_high, preferred_element_type=F32)
        low = jnp.dot(short, w_low, preferred_element_type=F32)
        if totals is None:
            return high, low
        return totals[0] + high, totals[1] + low

    def quad_lanes(quad):
        return pl.ds(pl.multiple_of(quad * 256, 256), 256)

    def direct(quad, dist, later, later_dist):
        totals = None
        weights = target_weights(later)
        for part in range(4):
            distances(later, part, weights, later_dist)
            totals = weigh(quad, part, dist, totals)
        high, low = totals
        near_sum = jnp.zeros((8, 256), F32)
        for j in range(4):
            block = high[16 * j:16 * j + 8] + high[16 * j + 8:16 * j + 16] + low[8 * j:8 * j + 8]
            near_sum = jnp.where(lane_block == j, block, near_sum)
        near_sum = near_sum + pltpu.roll(near_sum, 4, 0)
        lanes = quad_lanes(quad)
        centre = pos_ref[:, lanes] - 0.5
        out_ref[:, lanes] = near_sum[0:3] - centre * near_sum[3:4]

    def gather(slot, part, start, count, picked, after=None):
        rows = rows_smem[slot]
        for k in range(start, start + count):
            row = table_ref[rows[part, k]]
            if after is not None and k == start + count - 1:
                row = row + after * 0.0
            picked[part, k:k + 1, :] = row
        return row

    def cell_features(quad, part, picked, feat_ref):
        turned = picked[part].T
        lane_group = cells_ref[pl.ds(4 * quad + part, 1), :]
        feat = turned[0:16]
        for j in range(1, 8):
            feat = jnp.where(lane_group == j, turned[16 * j:16 * j + 16], feat)
        feat_ref[part] = feat

    def multipole(quad, part, start, feat_ref, pieces, after):
        first = (part % 2) * 64 + start
        xyz = columns[2 * quad + part // 2, first:first + CHUNK, :]
        feat = [feat_ref[part, f:f + 1, :] for f in range(10)]
        if after is not None:
            feat[9] = feat[9] + after * 0.0
        dx = xyz[:, 0:1] - feat[1]
        dy = xyz[:, 1:2] - feat[2]
        dz = xyz[:, 2:3] - feat[3]
        h = dx * dx + dy * dy + dz * dz + EPS
        inv = lax.rsqrt(h)
        inv2 = inv * inv
        inv5 = inv2 * inv2 * inv
        qx = feat[4] * dx + feat[7] * dy + feat[8] * dz
        qy = feat[7] * dx + feat[5] * dy + feat[9] * dz
        qz = feat[8] * dx + feat[9] * dy + feat[6] * dz
        form = dx * qx + dy * qy + dz * qz
        along = feat[0] * h + (2.5 * form) * inv2
        row = part * 64 + start
        for c, (d, q) in enumerate(((dx, qx), (dy, qy), (dz, qz))):
            high, low = split2(inv5 * (q - along * d))
            pieces[row:row + CHUNK, 256 * c:256 * c + 128] = high
            pieces[row:row + CHUNK, 256 * c + 128:256 * c + 256] = low
        return inv5[0:1] * along[0:1]

    def cells_pull(quad, feat_ref, pieces, later, slot, later_picked, later_feat, after):
        steps = LEAF // CHUNK
        fetched, summed = after
        for part in range(4):
            for c in range(steps):
                back = summed[-LAG] if len(summed) >= LAG else None
                row = gather(slot, part, c * (NCELL // steps), NCELL // steps, later_picked, back)
                summed = summed + [multipole(quad, part, c * CHUNK, feat_ref, pieces, fetched)]
                fetched = row
            cell_features(later, part, later_picked, later_feat)
        far_sum = nt(summing, pieces[...])
        lanes = quad_lanes(quad)
        out_ref[:, lanes] = out_ref[:, lanes] + far_sum[0:3]
        return fetched, summed

    quads = PAIRS // 2
    first_weights = target_weights(0)
    for part in range(4):
        distances(0, part, first_weights, dist_a)

    def direct_four(i, _):
        for when, stage in STAGE_AT:
            @pl.when(i == when)
            def _():
                finish_stage(stage)
                start_stage(stage + 1)
        for j in range(0, 4, 2):
            quad = 4 * i + j
            direct(quad, dist_a, quad + 1, dist_b)
            direct(quad + 1, dist_b, jnp.minimum(quad + 2, quads - 1), dist_a)
        return 0

    lax.fori_loop(0, quads // 4, direct_four, 0)
    finish_stage(3)
    row_copy(0, N_SLOTS - 1).wait()
    for part in range(4):
        gather(N_SLOTS - 1, part, 0, NCELL, picked_a)
        cell_features(0, part, picked_a, feat_a)
    row_copy(N_SLOTS, N_SLOTS - 1).start()

    def cells_some(i, _):
        for block in range(0, N_SLOTS, 4):
            for slot in range(block, block + 4):
                row_copy(0, slot).wait()
            after = (None, [])
            for slot in range(block, block + 4):
                quad = N_SLOTS * i + slot
                later = jnp.minimum(quad + 1, quads - 1)
                if slot % 2 == 0:
                    after = cells_pull(quad, feat_a, pieces_a, later, slot, picked_b, feat_b, after)
                else:
                    after = cells_pull(quad, feat_b, pieces_b, later, slot, picked_a, feat_a, after)
            for slot in range(block, block + 4):
                row_copy(jnp.minimum(N_SLOTS * (i + 1) + slot + 1, quads - 1), slot).start()
        return 0

    lax.fori_loop(0, quads // N_SLOTS, cells_some, 0)
    for slot in range(N_SLOTS):
        row_copy(0, slot).wait()

    for copy in near + far:
        copy.wait_send()
    for stage in range(3):
        for part in range(n_parts):
            for copy in stage_copies(part, stage):
                copy.wait_send()
    for part in range(n_parts):
        core_copy(part).wait_send()


def on_device(
    positions, masses, cell_mass, cell_center, cell_quad, cell_list, leaf_list, send_list, send_count,
):
    dma = pltpu.SemaphoreType.DMA
    n_off = len(OFFSETS)
    n_parts = len(PARTS)
    return pl.pallas_call(
        kernel,
        name="tree_pull",
        out_shape=jax.ShapeDtypeStruct((3, PAIRS * 128), F32),
        in_specs=[pl.BlockSpec(memory_space=pl.ANY)] * 9,
        out_specs=pl.BlockSpec(memory_space=pltpu.VMEM),
        scratch_shapes=[
            pltpu.VMEM((3, PAIRS * 128), F32),
            pltpu.VMEM((PAIRS, 128), F32),
            pltpu.VMEM((1, 128), F32),
            pltpu.VMEM((3, 128), F32),
            pltpu.VMEM((6, 128), F32),
            pltpu.VMEM((128, 128), jnp.int32),
            pltpu.SMEM((NLEAF, 128), jnp.int32),
            pltpu.SMEM((n_off, CAP), jnp.int32),
            pltpu.SMEM((n_off,), jnp.int32),
            pltpu.VMEM((128, 128), F32),
            pltpu.VMEM((PAIRS, 4, 128), F32),
            pltpu.VMEM((n_off, CAP // 2, 4, 128), F32),
            pltpu.VMEM((ALL_PAIRS, 4, 128), F32),
            pltpu.VMEM((N_CELL_ROWS, 1, 128), F32),
            pltpu.VMEM((2 * ALL_PAIRS, 64, 128), BF16),
            pltpu.VMEM((2 * ALL_PAIRS, 16, 128), BF16),
            pltpu.VMEM((PAIRS, 64, 128), BF16),
            pltpu.VMEM((PAIRS, 128, 8), F32),
            pltpu.VMEM((PAIRS // 2, 4, 128), jnp.int32),
            [pltpu.SMEM((4, 128), jnp.int32) for _ in range(N_SLOTS)],
            pltpu.VMEM((4, 128, 128), F32),
            pltpu.VMEM((4, 128, 128), F32),
            pltpu.VMEM((4, 16, 128), F32),
            pltpu.VMEM((4, 16, 128), F32),
            pltpu.VMEM((256, 768), BF16),
            pltpu.VMEM((256, 768), BF16),
            pltpu.VMEM((4, 256, 256), F32),
            pltpu.VMEM((4, 256, 256), F32),
            dma((9,)), dma((N_SLOTS,)),
            dma((NY,)), dma((NY,)), dma((n_off,)), dma((n_off,)),
            dma((n_parts, 3, NZ)), dma((n_parts, 3, NZ)), dma((n_parts,)), dma((n_parts,)),
        ],
        compiler_params=pltpu.CompilerParams(
            collective_id=0, has_side_effects=True, vmem_limit_bytes=60 * 1024 * 1024),
    )(
        positions, masses.reshape(PAIRS, 128), cell_mass.reshape(1, 128), cell_center, cell_quad,
        cell_list, leaf_list.T, send_list.reshape(2 * RANGE, CAP), send_count.reshape(2 * RANGE))


def solution(mesh):
    return jax.shard_map(
        on_device,
        mesh=mesh,
        in_specs=(
            P(None, ("dom", "sub")),
            P(("dom", "sub")),
            P(("dom", "sub")),
            P(None, ("dom", "sub")),
            P(None, ("dom", "sub")),
            P(("dom", "sub"), None),
            P(("dom", "sub"), None),
            P("dom", "sub", None, None),
            P("dom", "sub", None),
        ),
        out_specs=P(None, ("dom", "sub")),
        check_vma=False,
    )
```

```python
import functools

import jax
import jax.numpy as jnp
from jax import lax
from jax.experimental import pallas as pl
from jax.experimental.pallas import tpu as pltpu
from jax.sharding import PartitionSpec as P

LEAF = 64
NCELL = 128
NLEAF = 16
RANGE = 4
CAP = 8
EPS = 0.0025
F32 = jnp.float32
BF16 = jnp.bfloat16
MESH = pl.DeviceIdType.MESH

NX, NY, NZ, NCORE = 4, 4, 8, 2
SIZES = {"x": NX, "y": NY, "z": NZ}
ROWS = 16
PARTS = ((0, 8, ("z", "x", "y")), (8, 8, ("z", "y", "x")))
OFFSETS = tuple(range(-RANGE, 0)) + tuple(range(1, RANGE + 1))
PAIRS = 64
ALL_PAIRS = NY * PAIRS + len(OFFSETS) * CAP // 2
N_CELL_ROWS = NX * NY * NZ * NCORE * ROWS
N_SLOTS = 8
LAG = 2
CHUNK = 32
STAGE_AT = ((4, 2),)


def split3(value):
    high = value.astype(BF16).astype(F32)
    rest = value - high
    mid = rest.astype(BF16).astype(F32)
    return high, mid, rest - mid


def split2(value):
    high = value.astype(BF16)
    return high, (value - high.astype(F32)).astype(BF16)


def nt(a, b):
    return lax.dot_general(a, b, (((1,), (1,)), ((), ())), preferred_element_type=F32)


def cell_row(cell):
    shard = cell // 128
    sub = shard % NY
    dom = shard // NY
    at = {"x": dom // (NZ * NCORE), "z": (dom // NCORE) % NZ, "y": sub}
    core = dom % NCORE
    row = cell % 16
    n = N_CELL_ROWS // ROWS
    result = None
    for first, rows, order in PARTS:
        index, stride = 0, 1
        for axis in order:
            index = index + at[axis] * stride
            stride = stride * SIZES[axis]
        index = index + core * stride
        here = n * first + index * rows + (row - first)
        result = here if result is None else jnp.where(row >= first, here, result)
    return result


def kernel(
    pos_hbm, mass_hbm, cmass_hbm, ccen_hbm, cquad_hbm, cells_hbm, leaf_hbm, list_hbm, count_hbm,
    out_ref,
    pos_ref, mass_ref, cmass_ref, ccen_ref, cquad_ref, cells_ref, leaf_ids, send_list, send_count,
    pad, own, far_out, leaf_ref, table_ref,
    features, moments, targets, columns, rows_vmem, rows_smem, picked_a, picked_b, feat_a, feat_b, pieces_a, pieces_b,
    dist_a, dist_b,
    load_sem, row_sem, near_send, near_recv, far_send, far_recv, cell_send, cell_recv, core_send, core_recv,
):
    dom = lax.axis_index("dom")
    sub = lax.axis_index("sub")
    core = dom % NCORE
    at = {"x": dom // (NZ * NCORE), "z": (dom // NCORE) % NZ, "y": sub}
    n_dom = NX * NZ * NCORE
    base = sub * PAIRS

    loads = [
        pltpu.make_async_copy(src, dst, load_sem.at[i])
        for i, (src, dst) in enumerate((
            (pos_hbm, pos_ref), (mass_hbm, mass_ref), (cmass_hbm, cmass_ref), (ccen_hbm, ccen_ref),
            (cquad_hbm, cquad_ref), (list_hbm, send_list), (count_hbm, send_count), (cells_hbm, cells_ref),
            (leaf_hbm, leaf_ids)))
    ]
    for load in loads:
        load.start()

    def device(x, y, z, c):
        return ((x * NZ + z) * NCORE + c, y)

    def peer(axis, step):
        where = dict(at)
        where[axis] = (at[axis] + step) % SIZES[axis]
        return device(where["x"], where["y"], where["z"], core)

    barrier = pltpu.get_barrier_semaphore()
    waits = 0
    for axis in ("x", "y", "z"):
        for step in range(1, SIZES[axis]):
            pl.semaphore_signal(barrier, inc=1, device_id=peer(axis, step), device_id_type=MESH)
            waits += 1
    other_core = device(at["x"], at["y"], at["z"], 1 - core)
    pl.semaphore_signal(barrier, inc=1, device_id=other_core, device_id_type=MESH)
    waits += 1
    for off in OFFSETS:
        pl.semaphore_signal(barrier, inc=1, device_id=((dom + off + n_dom) % n_dom, sub), device_id_type=MESH)
        waits += 1

    for load in loads[0:5]:
        load.wait()
    for j in range(PAIRS):
        own[j, 0:3, :] = pos_ref[:, j * 128:(j + 1) * 128]
        own[j, 3:4, :] = mass_ref[j:j + 1, :]
    pad[...] = jnp.zeros((128, 128), F32)
    pad[0:1, :] = cmass_ref[...]
    pad[1:4, :] = ccen_ref[...]
    pad[4:10, :] = cquad_ref[...]
    by_cell = pad[...].T
    packed = by_cell[0:16, :]
    for g in range(1, 8):
        packed = packed + pltpu.roll(by_cell[16 * g:16 * g + 16, :], 16 * g, 1)
    pad[0:16, :] = packed

    def start_of(part, done):
        first, rows, order = PARTS[part]
        size = rows
        n = N_CELL_ROWS // ROWS
        index = 0
        stride = 1
        for s, axis in enumerate(order):
            if s >= done:
                index = index + at[axis] * stride
            stride = stride * SIZES[axis]
        index = index + core * stride
        for axis in order[:done]:
            size = size * SIZES[axis]
        return n * first + index * rows, size

    for part, (first, rows, order) in enumerate(PARTS):
        start, _ = start_of(part, 0)
        for r in range(rows):
            table_ref[start + r, :, :] = pad[first + r:first + r + 1, :]

    row8 = lax.broadcasted_iota(jnp.int32, (8, 128), 0)
    one_row = jnp.where(row8 == 4, 1.0, 0.0).astype(F32)
    no_rows = jnp.zeros((16, 128), F32)

    def prepare(source_ref, source, pair):
        raw4 = source_ref[source]
        raw = jnp.concatenate([raw4, raw4], axis=0)
        mass = raw4[3:4, :]
        centred = raw - 0.5
        square = jnp.where(row8 < 3, centred * centred, 0.0)
        norm = jnp.sum(square, axis=0, keepdims=True) + EPS
        u = jnp.where(row8 < 3, centred, jnp.where(row8 == 3, norm, one_row))
        s = jnp.where(row8 < 3, centred * mass, jnp.where(row8 == 3, mass, 0.0))
        u_high, u_mid, u_low = split3(u)
        s_high, s_mid, s_low = split3(s)
        s_full = jnp.concatenate([s_high + pltpu.roll(s_mid, 4, 0), s_low], axis=0)
        moments[2 * pair] = s_full.astype(BF16)
        moments[2 * pair + 1] = pltpu.roll(s_full, LEAF, 1).astype(BF16)
        u_full = jnp.concatenate([u_high, u_mid, u_high, u_mid, u_high, u_low, no_rows], axis=0).astype(BF16)
        turned = jnp.concatenate([u_full, u_full], axis=0).T
        features[2 * pair] = turned[0:64]
        features[2 * pair + 1] = turned[64:128]

    def prepare_range(source_ref, source, pair, count):
        def body(j, _):
            prepare(source_ref, source + j, pair + j)
            return 0
        lax.fori_loop(0, count, body, 0, unroll=16)

    def prepare_targets(pair, _):
        raw3 = pos_ref[:, pl.ds(pl.multiple_of(pair * 128, 128), 128)]
        raw = jnp.concatenate([raw3, jnp.zeros((5, 128), F32)], axis=0)
        centred = raw - 0.5
        square = jnp.where(row8 < 3, centred * centred, 0.0)
        norm = jnp.sum(square, axis=0, keepdims=True)
        t = jnp.where(row8 < 3, -2.0 * centred,
                      jnp.where(row8 == 3, 1.0, jnp.where(row8 == 4, norm, 0.0)))
        t_high, t_mid, t_low = split3(t)
        targets[pair] = jnp.concatenate(
            [t_high, t_high, t_mid, t_mid, t_low, t_high, no_rows], axis=0).astype(BF16)
        columns[pair] = jnp.concatenate([raw, jnp.zeros((120, 128), F32)], axis=0).T[:, 0:8]
        return 0

    prepare_range(own, 0, base, PAIRS)
    lax.fori_loop(0, PAIRS, prepare_targets, 0, unroll=8)
    for load in loads[7:9]:
        load.wait()
    cells = cells_ref[...]
    found = cell_row(cells)
    for quad in range(PAIRS // 2):
        rows_vmem[quad] = found[4 * quad:4 * quad + 4]
    cells_ref[...] = (cells >> 4) & 7

    def row_copy(quad, slot):
        return pltpu.make_async_copy(rows_vmem.at[quad], rows_smem[slot], row_sem.at[slot])

    row_copy(0, N_SLOTS - 1).start()
    for slot in range(N_SLOTS - 1):
        row_copy(slot + 1, slot).start()

    pl.semaphore_wait(barrier, waits)

    def cell_copy(part, stage, step):
        axis = PARTS[part][2][stage]
        start, size = start_of(part, stage)
        block = table_ref.at[pl.ds(start, size)]
        return pltpu.make_async_remote_copy(
            src_ref=block, dst_ref=block,
            send_sem=cell_send.at[part, stage, step], recv_sem=cell_recv.at[part, stage, step],
            device_id=peer(axis, step), device_id_type=MESH)

    def stage_copies(part, stage):
        return [cell_copy(part, stage, step) for step in range(1, SIZES[PARTS[part][2][stage]])]

    def core_copy(part):
        start, size = start_of(part, 3)
        block = table_ref.at[pl.ds(start, size)]
        return pltpu.make_async_remote_copy(
            src_ref=block, dst_ref=block, send_sem=core_send.at[part], recv_sem=core_recv.at[part],
            device_id=other_core, device_id_type=MESH)

    n_parts = len(PARTS)

    def start_stage(stage):
        for part in range(n_parts):
            if stage == 3:
                core_copy(part).start()
            else:
                for copy in stage_copies(part, stage):
                    copy.start()

    def finish_stage(stage):
        for part in range(n_parts):
            if stage == 3:
                core_copy(part).wait_recv()
            else:
                for copy in stage_copies(part, stage):
                    copy.wait_recv()

    near = [
        pltpu.make_async_remote_copy(
            src_ref=own, dst_ref=leaf_ref.at[pl.ds(base, PAIRS)],
            send_sem=near_send.at[step], recv_sem=near_recv.at[step],
            device_id=peer("y", step), device_id_type=MESH)
        for step in range(1, NY)
    ]
    for copy in near:
        copy.start()
    start_stage(0)

    for load in loads[5:7]:
        load.wait()
    low_half4 = lax.broadcasted_iota(jnp.int32, (4, 128), 1) < LEAF

    def far_pair(slot, t):
        halves = []
        for h in range(2):
            block = send_list[slot, 2 * t + h]
            tile = own[block // 2]
            turned = pltpu.roll(tile, LEAF, 1)
            picked = jnp.where(block % 2 == h, tile, turned)
            inside = jnp.logical_and(dom + OFFSETS[slot] >= 0, dom + OFFSETS[slot] < n_dom)
            live = jnp.logical_and(inside, 2 * t + h < send_count[slot])
            halves.append(jnp.where(live, picked, jnp.zeros_like(picked)))
        far_out[slot, t] = jnp.where(low_half4, halves[0], halves[1])

    def far_copy(slot):
        return pltpu.make_async_remote_copy(
            src_ref=far_out.at[slot],
            dst_ref=leaf_ref.at[pl.ds(NY * PAIRS + slot * (CAP // 2), CAP // 2)],
            send_sem=far_send.at[slot], recv_sem=far_recv.at[slot],
            device_id=((dom + OFFSETS[slot] + n_dom) % n_dom, sub), device_id_type=MESH)

    for slot in range(len(OFFSETS)):
        for t in range(CAP // 2):
            far_pair(slot, t)
    far = [far_copy(slot) for slot in range(len(OFFSETS))]
    for copy in far:
        copy.start()

    finish_stage(0)
    start_stage(1)
    for copy in far:
        copy.wait_recv()
    prepare_range(leaf_ref, NY * PAIRS, NY * PAIRS, len(OFFSETS) * CAP // 2)
    for step in range(1, NY):
        near[step - 1].wait_recv()
        if step == NY - 1:
            finish_stage(1)
            start_stage(2)
        origin = ((sub + NY - step) % NY) * PAIRS
        prepare_range(leaf_ref, origin, origin, PAIRS)

    low_half = lax.broadcasted_iota(jnp.int32, (64, 128), 1) < LEAF
    low_half16 = lax.broadcasted_iota(jnp.int32, (16, 128), 1) < LEAF
    summing_row = lax.broadcasted_iota(jnp.int32, (8, 768), 0)
    summing_lane = lax.broadcasted_iota(jnp.int32, (8, 768), 1)
    summing = jnp.where(summing_row == (summing_lane // 256), 1.0, 0.0).astype(BF16)
    lane_block = lax.broadcasted_iota(jnp.int32, (8, 256), 1) // LEAF
    nothing = jnp.zeros((64, 128), BF16)
    empty = jnp.zeros((128, 128), BF16)

    def target_weights(quad):
        blocks = []
        for half in range(2):
            tile = targets[2 * quad + half]
            diagonal = jnp.concatenate(
                [jnp.where(low_half, tile, nothing), jnp.where(low_half, nothing, tile)], axis=0)
            blocks.append(jnp.concatenate([diagonal, empty] if half == 0 else [empty, diagonal], axis=0))
        return jnp.concatenate(blocks, axis=1)

    def distances(quad, part, weights, dist):
        rows = []
        for slot in range(4 * part, 4 * part + 4):
            halves = []
            for half in range(2):
                first = leaf_ids[slot, 4 * quad + 2 * half]
                second = leaf_ids[slot, 4 * quad + 2 * half + 1]
                halves.append(jnp.where(low_half, features[first], features[second]))
            rows.append(jnp.concatenate(halves, axis=1))
        lhs = jnp.concatenate(rows, axis=0)
        dist[part] = jnp.dot(lhs, weights, preferred_element_type=F32)

    def weigh(quad, part, dist, totals):
        inv = lax.rsqrt(dist[part])
        w_high, w_low = split2(inv * inv * inv)
        rows = []
        for j in range(4):
            group = 4 * quad + j
            tiles = []
            for slot in range(4 * part, 4 * part + 4, 2):
                low = leaf_ids[slot, group]
                high = leaf_ids[slot + 1, group]
                tiles.append(jnp.where(low_half16, moments[low], moments[high ^ 1]))
            rows.append(jnp.concatenate(tiles, axis=1))
        full = jnp.concatenate(rows, axis=0)
        short = jnp.concatenate([row[0:8] for row in rows], axis=0)
        high = jnp.dot(full, w_high, preferred_element_type=F32)
        low = jnp.dot(short, w_low, preferred_element_type=F32)
        if totals is None:
            return high, low
        return totals[0] + high, totals[1] + low

    def quad_lanes(quad):
        return pl.ds(pl.multiple_of(quad * 256, 256), 256)

    def direct(quad, dist, later, later_dist):
        totals = None
        weights = target_weights(later)
        for part in range(4):
            distances(later, part, weights, later_dist)
            totals = weigh(quad, part, dist, totals)
        high, low = totals
        near_sum = jnp.zeros((8, 256), F32)
        for j in range(4):
            block = high[16 * j:16 * j + 8] + high[16 * j + 8:16 * j + 16] + low[8 * j:8 * j + 8]
            near_sum = jnp.where(lane_block == j, block, near_sum)
        near_sum = near_sum + pltpu.roll(near_sum, 4, 0)
        lanes = quad_lanes(quad)
        centre = pos_ref[:, lanes] - 0.5
        out_ref[:, lanes] = near_sum[0:3] - centre * near_sum[3:4]

    def gather(slot, part, start, count, picked, after=None):
        rows = rows_smem[slot]
        for k in range(start, start + count):
            row = table_ref[rows[part, k]]
            if after is not None and k == start + count - 1:
                row = row + after * 0.0
            picked[part, k:k + 1, :] = row
        return row

    def cell_features(quad, part, picked, feat_ref):
        turned = picked[part].T
        lane_group = cells_ref[pl.ds(4 * quad + part, 1), :]
        feat = turned[0:16]
        for j in range(1, 8):
            feat = jnp.where(lane_group == j, turned[16 * j:16 * j + 16], feat)
        feat_ref[part] = feat

    def multipole(quad, part, start, feat_ref, pieces, after):
        first = (part % 2) * 64 + start
        xyz = columns[2 * quad + part // 2, first:first + CHUNK, :]
        feat = [feat_ref[part, f:f + 1, :] for f in range(10)]
        if after is not None:
            feat[9] = feat[9] + after * 0.0
        dx = xyz[:, 0:1] - feat[1]
        dy = xyz[:, 1:2] - feat[2]
        dz = xyz[:, 2:3] - feat[3]
        h = dx * dx + dy * dy + dz * dz + EPS
        inv = lax.rsqrt(h)
        inv2 = inv * inv
        inv5 = inv2 * inv2 * inv
        qx = feat[4] * dx + feat[7] * dy + feat[8] * dz
        qy = feat[7] * dx + feat[5] * dy + feat[9] * dz
        qz = feat[8] * dx + feat[9] * dy + feat[6] * dz
        form = dx * qx + dy * qy + dz * qz
        along = feat[0] * h + (2.5 * form) * inv2
        row = part * 64 + start
        for c, (d, q) in enumerate(((dx, qx), (dy, qy), (dz, qz))):
            high, low = split2(inv5 * (q - along * d))
            pieces[row:row + CHUNK, 256 * c:256 * c + 128] = high
            pieces[row:row + CHUNK, 256 * c + 128:256 * c + 256] = low
        return inv5[0:1] * along[0:1]

    def cells_pull(quad, feat_ref, pieces, later, slot, later_picked, later_feat, after):
        steps = LEAF // CHUNK
        fetched, summed = after
        for part in range(4):
            for c in range(steps):
                back = summed[-LAG] if len(summed) >= LAG else None
                row = gather(slot, part, c * (NCELL // steps), NCELL // steps, later_picked, back)
                summed = summed + [multipole(quad, part, c * CHUNK, feat_ref, pieces, fetched)]
                fetched = row
            cell_features(later, part, later_picked, later_feat)
        far_sum = nt(summing, pieces[...])
        lanes = quad_lanes(quad)
        out_ref[:, lanes] = out_ref[:, lanes] + far_sum[0:3]
        return fetched, summed

    quads = PAIRS // 2
    first_weights = target_weights(0)
    for part in range(4):
        distances(0, part, first_weights, dist_a)

    def direct_four(i, _):
        for when, stage in STAGE_AT:
            @pl.when(i == when)
            def _():
                finish_stage(stage)
                start_stage(stage + 1)
        for j in range(0, 4, 2):
            quad = 4 * i + j
            direct(quad, dist_a, quad + 1, dist_b)
            direct(quad + 1, dist_b, jnp.minimum(quad + 2, quads - 1), dist_a)
        return 0

    lax.fori_loop(0, quads // 4, direct_four, 0)
    finish_stage(3)
    row_copy(0, N_SLOTS - 1).wait()
    for part in range(4):
        gather(N_SLOTS - 1, part, 0, NCELL, picked_a)
        cell_features(0, part, picked_a, feat_a)
    row_copy(N_SLOTS, N_SLOTS - 1).start()

    def cells_some(i, _):
        for block in range(0, N_SLOTS, 4):
            for slot in range(block, block + 4):
                row_copy(0, slot).wait()
            after = (None, [])
            for slot in range(block, block + 4):
                quad = N_SLOTS * i + slot
                later = jnp.minimum(quad + 1, quads - 1)
                if slot % 2 == 0:
                    after = cells_pull(quad, feat_a, pieces_a, later, slot, picked_b, feat_b, after)
                else:
                    after = cells_pull(quad, feat_b, pieces_b, later, slot, picked_a, feat_a, after)
            for slot in range(block, block + 4):
                row_copy(jnp.minimum(N_SLOTS * (i + 1) + slot + 1, quads - 1), slot).start()
        return 0

    lax.fori_loop(0, quads // N_SLOTS, cells_some, 0)
    for slot in range(N_SLOTS):
        row_copy(0, slot).wait()

    for copy in near + far:
        copy.wait_send()
    for stage in range(3):
        for part in range(n_parts):
            for copy in stage_copies(part, stage):
                copy.wait_send()
    for part in range(n_parts):
        core_copy(part).wait_send()


def on_device(
    positions, masses, cell_mass, cell_center, cell_quad, cell_list, leaf_list, send_list, send_count,
):
    dma = pltpu.SemaphoreType.DMA
    n_off = len(OFFSETS)
    n_parts = len(PARTS)
    return pl.pallas_call(
        kernel,
        name="tree_pull",
        out_shape=jax.ShapeDtypeStruct((3, PAIRS * 128), F32),
        in_specs=[pl.BlockSpec(memory_space=pl.ANY)] * 9,
        out_specs=pl.BlockSpec(memory_space=pltpu.VMEM),
        scratch_shapes=[
            pltpu.VMEM((3, PAIRS * 128), F32),
            pltpu.VMEM((PAIRS, 128), F32),
            pltpu.VMEM((1, 128), F32),
            pltpu.VMEM((3, 128), F32),
            pltpu.VMEM((6, 128), F32),
            pltpu.VMEM((128, 128), jnp.int32),
            pltpu.SMEM((NLEAF, 128), jnp.int32),
            pltpu.SMEM((n_off, CAP), jnp.int32),
            pltpu.SMEM((n_off,), jnp.int32),
            pltpu.VMEM((128, 128), F32),
            pltpu.VMEM((PAIRS, 4, 128), F32),
            pltpu.VMEM((n_off, CAP // 2, 4, 128), F32),
            pltpu.VMEM((ALL_PAIRS, 4, 128), F32),
            pltpu.VMEM((N_CELL_ROWS, 1, 128), F32),
            pltpu.VMEM((2 * ALL_PAIRS, 64, 128), BF16),
            pltpu.VMEM((2 * ALL_PAIRS, 16, 128), BF16),
            pltpu.VMEM((PAIRS, 64, 128), BF16),
            pltpu.VMEM((PAIRS, 128, 8), F32),
            pltpu.VMEM((PAIRS // 2, 4, 128), jnp.int32),
            [pltpu.SMEM((4, 128), jnp.int32) for _ in range(N_SLOTS)],
            pltpu.VMEM((4, 128, 128), F32),
            pltpu.VMEM((4, 128, 128), F32),
            pltpu.VMEM((4, 16, 128), F32),
            pltpu.VMEM((4, 16, 128), F32),
            pltpu.VMEM((256, 768), BF16),
            pltpu.VMEM((256, 768), BF16),
            pltpu.VMEM((4, 256, 256), F32),
            pltpu.VMEM((4, 256, 256), F32),
            dma((9,)), dma((N_SLOTS,)),
            dma((NY,)), dma((NY,)), dma((n_off,)), dma((n_off,)),
            dma((n_parts, 3, NZ)), dma((n_parts, 3, NZ)), dma((n_parts,)), dma((n_parts,)),
        ],
        compiler_params=pltpu.CompilerParams(
            collective_id=0, has_side_effects=True, vmem_limit_bytes=60 * 1024 * 1024),
    )(
        positions, masses.reshape(PAIRS, 128), cell_mass.reshape(1, 128), cell_center, cell_quad,
        cell_list, leaf_list.T, send_list.reshape(2 * RANGE, CAP), send_count.reshape(2 * RANGE))


def solution(mesh):
    return jax.shard_map(
        on_device,
        mesh=mesh,
        in_specs=(
            P(None, ("dom", "sub")),
            P(("dom", "sub")),
            P(("dom", "sub")),
            P(None, ("dom", "sub")),
            P(None, ("dom", "sub")),
            P(("dom", "sub"), None),
            P(("dom", "sub"), None),
            P("dom", "sub", None, None),
            P("dom", "sub", None),
        ),
        out_specs=P(None, ("dom", "sub")),
        check_vma=False,
    )
```
